32 devices in a mesh: series: 8 (over z, y), tm: 4 (over x, core).
Axes of the slice: x: 2, y: 2, z: 4, core: 2. Of those that a mesh axis runs over, the one named last changes fastest.
Arguments:
- observed: bfloat16 [131072, 2048], P('series', 'tm'), may hold values from -6 to 6
- flags: int32 [131072, 16], P('series', 'tm'), may hold values 0 or 1
- factors: bfloat16 [131072, 64], P('series'), may hold values from -0.75 to 0.75
- basis: float32 [64, 2048], P(None, 'tm'), may hold values from -6 to 6
- tcn_weights: float32 [4, 64, 64], replicated, may hold values from -0.5 to 0.5
- tcn_bias: float32 [2, 64], replicated, may hold values from -3 to 3
- dilations: int32 [2], replicated, may hold values from 1 to 64, as said below
Outputs:
- new_basis: float32 [64, 2048], P(None, 'tm')
- new_factors: bfloat16 [131072, 64], P('series')
The draws below stay inside these ranges and needn't reach their ends.
Inputs may be any that keep to these rules, and one draw needn't show every extreme that they name: `dilations`: each dilation is between 1 and 64, and at least one of the two equals 64.
All inputs are finite; a program needn't handle non-finite values. No bound on the sum of `flags` on one device may be relied on, other than what follows from the above.
Results may differ from the reference program's by a relative error of at most 0.002.
The reference program's roundings to bfloat16 on the way (of `resid`) count: a program that leaves them out, or rounds other values in their place, can miss the bound.
Values may be sent and summed in bfloat16 or wider, within the bound.
No kernel may reach another device: no remote copies, remote signals or barrier semaphores. Data moves between devices by JAX's collectives and lax.ppermute only.
A program may use at most 192 MiB of HBM per device.

```python
import math
import jax
import jax.numpy as jnp
from jax import lax

K = 64
R_DEV = 16384
DMAX = 64
BLK = 128
ITERS = 3
HALO = 129
NSERIES = 131072
TT = 2048


def draw_dilations(key, part):
    first_key = jax.random.fold_in(key, 11)
    order_key = jax.random.fold_in(key, 12)
    other = jax.random.randint(first_key, (1,), 1, DMAX + 1).astype(jnp.int32)
    both = jnp.concatenate([other, jnp.full((1,), DMAX, jnp.int32)])
    order = jax.random.permutation(order_key, 2)
    return both[order].astype(jnp.int32)


def draw_factors(key, part):
    base_key = jax.random.fold_in(key, 21)
    shared_key = jax.random.fold_in(key, 22)
    level_key = jax.random.fold_in(key, 23)
    blocks = NSERIES // R_DEV
    base = jax.random.normal(base_key, (NSERIES, K), jnp.float32)
    shared = jax.random.normal(shared_key, (NSERIES, 1), jnp.float32)
    levels = jnp.exp(jax.random.uniform(level_key, (blocks, K), jnp.float32, -0.7, 0.7))
    column_scale = jnp.repeat(levels, R_DEV, axis=0)
    values = 0.15 * shared + base * column_scale * (1.0 / math.sqrt(K))
    return jnp.clip(values, -0.75, 0.75).astype(jnp.bfloat16)


def set_ends(array, own_key, smallest, high):
    place = [jax.random.randint(jax.random.fold_in(own_key, axis), (), 0, length) for axis, length in enumerate(array.shape)]
    longest = array.shape.index(max(array.shape))
    neighbour = place[:longest] + [(place[longest] + 1) % array.shape[longest]] + place[longest + 1:]
    return array.at[tuple(place)].set(smallest).at[tuple(neighbour)].set(high)


def steps_of(own_key, dims, pieces, smallest, top_value):
    def one(dim, parts):
        heights = jax.random.uniform(jax.random.fold_in(jax.random.fold_in(own_key, 6), dim), (parts,), jnp.float32, smallest / len(pieces), top_value / len(pieces))
        return jnp.repeat(jnp.exp(heights), dims[dim] // parts).reshape((-1,) + (1,) * (len(dims) - dim - 1))

    level = one(*pieces[0])
    for cut in pieces[1:]:
        level = level * one(*cut)
    return level


def centred(own_key, shape, spread, most, cuts=(), held_as=jnp.bfloat16):
    factor_of = steps_of(own_key, shape, cuts, -0.22, 0.18) if cuts else 1.0
    array = jax.random.normal(own_key, shape, jnp.float32) * spread * factor_of
    return jnp.minimum(jnp.maximum(array, -most), most).astype(held_as)


def setup_inputs(seed: int = 0) -> dict:
    arg_keys = jax.random.split(jax.random.key(seed), 8)
    observed = centred(arg_keys[0], (NSERIES, TT), 1.0, 6.0, ((0, 8), (1, 4)))
    flags = set_ends((jax.random.randint(arg_keys[1], (NSERIES, TT // BLK), 0, 4) < 3).astype(jnp.int32), jax.random.fold_in(arg_keys[1], 1), 0, 1)
    factors = draw_factors(jax.random.fold_in(arg_keys[7], 71), 0)
    basis = centred(arg_keys[3], (K, TT), 1.0, 6.0, ((1, 4),), jnp.float32)
    tcn_weights = centred(arg_keys[4], (4, K, K), (2 * K) ** -0.5, 0.5, (), jnp.float32)
    tcn_bias = centred(arg_keys[5], (2, K), 0.5, 3.0, (), jnp.float32)
    dilations = draw_dilations(jax.random.fold_in(arg_keys[7], 71), 0)
    return dict(observed=observed, flags=flags, factors=factors, basis=basis, tcn_weights=tcn_weights, tcn_bias=tcn_bias, dilations=dilations)


def delay(field, steps):
    padded = jnp.pad(field, ((0, 0), (DMAX, 0)))
    return lax.dynamic_slice_in_dim(padded, (DMAX - steps).astype(jnp.int32), field.shape[1], 1)

def mix(weight, field):
    return jnp.dot(weight, field, precision=lax.Precision.HIGHEST)

def tcn_error(padded, tcn_weights, tcn_bias, dilations, keep):
    shifted = delay(padded, jnp.int32(1))
    hidden = jax.nn.relu(mix(tcn_weights[0], delay(shifted, dilations[0])) + mix(tcn_weights[1], shifted) + tcn_bias[0][:, None])
    output = mix(tcn_weights[2], delay(hidden, dilations[1])) + mix(tcn_weights[3], hidden) + tcn_bias[1][:, None]
    return (padded - shifted - output)[:, -keep:]

def resid_block(fac, obs, flg, basis_b):
    pred = jnp.dot(fac, basis_b, preferred_element_type=jnp.float32)
    diff = (pred - obs.astype(jnp.float32)).reshape(fac.shape[0], -1, BLK) * flg[:, :, None].astype(jnp.float32)
    return diff.reshape(fac.shape[0], -1).astype(jnp.bfloat16)

def reference(observed, flags, factors, basis, tcn_weights, tcn_bias, dilations):
    blocks = NSERIES // R_DEV
    fac_b = factors.reshape(blocks, R_DEV, K)
    obs_b = observed.reshape(blocks, R_DEV, TT)
    flg_b = flags.reshape(blocks, R_DEV, TT // BLK)
    current = basis
    for step in range(ITERS):
        basis_b = current.astype(jnp.bfloat16)

        def accumulate(total, item):
            fac, obs, flg = item
            resid = resid_block(fac, obs, flg, basis_b)
            return (total + lax.dot_general(fac, resid, (((0,), (0,)), ((), ())), preferred_element_type=jnp.float32), None)
        data_grad, unused = lax.scan(accumulate, jnp.zeros((K, TT), jnp.float32), (fac_b, obs_b, flg_b))
        padded = jnp.pad(current, ((0, 0), (HALO, 0)))
        error, pull = jax.vjp(lambda v: tcn_error(v, tcn_weights, tcn_bias, dilations, TT), padded)
        reg_grad = pull(0.1 * error)[0][:, HALO:]
        grad = data_grad * (1.0 / jnp.sqrt(jnp.float32(NSERIES))) + reg_grad
        norm = jnp.sqrt(jnp.mean(grad * grad) + 1e-06)
        current = current - 0.1 * grad / norm
    basis_b = current.astype(jnp.bfloat16)
    coef = 0.1 / jnp.sqrt(jnp.float32(TT))

    def update(item):
        fac, obs, flg = item
        resid = resid_block(fac, obs, flg, basis_b)
        fgrad = lax.dot_general(resid, basis_b, (((1,), (1,)), ((), ())), preferred_element_type=jnp.float32)
        return (fac.astype(jnp.float32) - coef * fgrad).astype(jnp.bfloat16)
    new_factors = lax.map(update, (fac_b, obs_b, flg_b)).reshape(NSERIES, K)
    return (current, new_factors)
```

```python
import math

import jax
import jax.numpy as jnp
from jax import lax
from jax.experimental import pallas as pl
from jax.experimental.pallas import tpu as pltpu
from jax.sharding import PartitionSpec as P

BLK = 128
LANES = 128
ITERS = 3
F32 = jnp.float32
BF16 = jnp.bfloat16
VMEM_BYTES = 48 << 20


def nt_dot(a, b):
    return lax.dot_general(a, b, (((1,), (1,)), ((), ())), preferred_element_type=F32)


def tn_dot(a, b):
    return lax.dot_general(a, b, (((0,), (0,)), ((), ())), preferred_element_type=F32)


def gram_kernel(obs_ref, fac_ref, flg_ref, out_ref):
    rank = fac_ref.shape[0]
    blocks = flg_ref.shape[0]
    fac = fac_ref[...]
    flg = flg_ref[...].astype(F32).astype(BF16)
    masked = jnp.concatenate([fac * flg[b : b + 1, :] for b in range(blocks)], axis=0)
    parts = []
    for b in range(0, blocks, 2):
        both = jnp.dot(
            masked[b * rank : (b + 2) * rank],
            obs_ref[:, b * BLK : (b + 2) * BLK],
            preferred_element_type=F32,
        )
        parts += [both[:rank, :BLK], both[rank:, BLK:]]
    new = jnp.concatenate(parts + [nt_dot(fac, masked)], axis=1)

    @pl.when(pl.program_id(0) == 0)
    def _():
        out_ref[...] = new

    @pl.when(pl.program_id(0) > 0)
    def _():
        out_ref[...] += new


def gram(observed, fac_t, flg_t, rows):
    series, cols = observed.shape
    rank, blocks = fac_t.shape[0], flg_t.shape[0]
    width = cols + blocks * rank
    return pl.pallas_call(
        gram_kernel,
        grid=(series // rows,),
        in_specs=[
            pl.BlockSpec((rows, cols), lambda i: (i, 0)),
            pl.BlockSpec((rank, rows), lambda i: (0, i)),
            pl.BlockSpec((blocks, rows), lambda i: (0, i)),
        ],
        out_specs=pl.BlockSpec((rank, width), lambda i: (0, 0)),
        out_shape=jax.ShapeDtypeStruct((rank, width), F32),
        compiler_params=pltpu.CompilerParams(vmem_limit_bytes=VMEM_BYTES),
        name="gram",
    )(observed, fac_t, flg_t)


def split(x):
    high = x.astype(BF16)
    return high, (x - high.astype(F32)).astype(BF16)


def later(x, steps, fill):
    lane = lax.broadcasted_iota(jnp.int32, (x.shape[0], LANES), 1)
    before = jnp.broadcast_to(fill, (x.shape[0], LANES))
    out = []
    for j in range(0, x.shape[1], LANES):
        rolled = pltpu.roll(x[:, j : j + LANES], steps, 1)
        out.append(jnp.where(lane < steps, before, rolled))
        before = rolled
    return jnp.concatenate(out, axis=1)


def earlier(x, steps):
    lane = lax.broadcasted_iota(jnp.int32, (x.shape[0], LANES), 1)
    rolled = [
        pltpu.roll(x[:, j : j + LANES], LANES - steps, 1) for j in range(0, x.shape[1], LANES)
    ]
    rolled.append(jnp.zeros((x.shape[0], LANES), F32))
    out = [jnp.where(lane < LANES - steps, a, b) for a, b in zip(rolled[:-1], rolled[1:])]
    return jnp.concatenate(out, axis=1)


def taps(first, second):
    fh, fl = split(first)
    sh, sl = split(second)
    zero = jnp.zeros_like(fh)
    top = jnp.concatenate([fh, sh, fh, sh], axis=1)
    bottom = jnp.concatenate([fl, sl, zero, zero], axis=1)
    return jnp.concatenate([top, bottom], axis=0)


def pair_dot(weights, a, b):
    ah, al = split(a)
    bh, bl = split(b)
    both = jnp.dot(
        weights, jnp.concatenate([ah, bh, al, bl], axis=0), preferred_element_type=F32
    )
    rank = a.shape[0]
    return both[:rank] + both[rank:]


def steps_kernel(
    dil_ref, place_ref, sums_ref, basis_ref, w_ref, bias_ref, basis_out, basis_b_out, x_ref,
    *, data_scale, entries
):
    rank, total = basis_ref.shape
    cols = basis_out.shape[1]
    slabs = total // cols
    d0, d1 = dil_ref[0], dil_ref[1]
    b0, b1 = bias_ref[:, 0:1], bias_ref[:, 1:2]
    w = [w_ref[i] for i in range(4)]
    layer1 = taps(w[0], w[1])
    layer2 = taps(w[2], w[3])
    back2 = taps(w[2].T, w[3].T)
    back1 = taps(w[0].T, w[1].T)
    x_ref[...] = basis_ref[...]

    def body(i, carry):
        x = x_ref[...]
        z = later(x, 1, 0.0)
        pre = pair_dot(layer1, later(z, d0, 0.0), z) + b0
        hidden = jnp.maximum(pre, 0.0)
        shown = later(hidden, d1, jnp.maximum(b0, 0.0))
        error = 0.1 * (x - z - pair_dot(layer2, shown, hidden) - b1)
        pull = -pair_dot(back2, earlier(error, d1), error)
        pull = jnp.where(pre > 0.0, pull, 0.0)
        reg = error + earlier(pair_dot(back1, earlier(pull, d0), pull) - error, 1)
        xb = x.astype(BF16)
        data = []
        for s in range(slabs):
            for b in range(0, cols // BLK, 2):
                at = s * cols + b * BLK
                pair = sums_ref[s, :, cols + b * rank : cols + (b + 2) * rank]
                high, rest = split(pair)
                mid = rest
                low = (pair - high.astype(F32) - mid.astype(F32)).astype(BF16)
                zero = jnp.zeros((rank, BLK), BF16)
                right = jnp.concatenate(
                    [
                        jnp.concatenate([xb[:, at : at + BLK], zero], axis=1),
                        jnp.concatenate([zero, xb[:, at + BLK : at + 2 * BLK]], axis=1),
                    ],
                    axis=0,
                )
                got = jnp.dot(
                    jnp.concatenate([high, mid, low], axis=0), right, preferred_element_type=F32
                )
                got = got[:rank] + (got[rank : 2 * rank] + got[2 * rank :])
                data.append(got - sums_ref[s, :, b * BLK : (b + 2) * BLK])
        grad = jnp.concatenate(data, axis=1) * data_scale + reg
        square = jnp.sum(grad * grad)
        x_ref[...] = x - grad * (0.1 * lax.rsqrt(jnp.full((1, 1), square) / entries + 1e-06))
        return carry

    lax.fori_loop(0, ITERS, body, 0)
    start = pl.multiple_of(place_ref[0] * cols, LANES)
    mine = x_ref[:, pl.ds(start, cols)]
    basis_out[...] = mine
    basis_b_out[...] = mine.astype(BF16)


def basis_steps(dilations, place, sums, basis_all, weights, bias_t, cols, data_scale):
    rank, total = basis_all.shape
    smem = pl.BlockSpec(memory_space=pltpu.SMEM)
    vmem = pl.BlockSpec(memory_space=pltpu.VMEM)
    return pl.pallas_call(
        lambda *refs: steps_kernel(*refs, data_scale=data_scale, entries=float(rank * total)),
        in_specs=[smem, smem, vmem, vmem, vmem, vmem],
        out_specs=[vmem, vmem],
        out_shape=[
            jax.ShapeDtypeStruct((rank, cols), F32),
            jax.ShapeDtypeStruct((rank, cols), BF16),
        ],
        scratch_shapes=[pltpu.VMEM((rank, total), F32)],
        compiler_params=pltpu.CompilerParams(vmem_limit_bytes=VMEM_BYTES),
        name="basis_steps",
    )(dilations, place, sums, basis_all, weights, bias_t)


def pull_kernel(obs_ref, fac_ref, flg_ref, basis_ref, out_ref):
    basis = basis_ref[...]
    flg = flg_ref[...].astype(F32)
    pred = tn_dot(fac_ref[...], basis)
    resid = (pred - obs_ref[...].astype(F32)).astype(BF16)
    total = None
    for b in range(flg.shape[0]):
        cut = slice(b * BLK, (b + 1) * BLK)
        term = nt_dot(basis[:, cut], resid[:, cut]) * flg[b : b + 1, :]
        total = term if total is None else total + term
    out_ref[...] = total


def factor_pull(observed, fac_t, flg_t, basis_b, first, series, rows):
    cols = observed.shape[1]
    rank, blocks = fac_t.shape[0], flg_t.shape[0]
    skip = first // rows
    return pl.pallas_call(
        pull_kernel,
        grid=(series // rows,),
        in_specs=[
            pl.BlockSpec((rows, cols), lambda i: (i + skip, 0)),
            pl.BlockSpec((rank, rows), lambda i: (0, i + skip)),
            pl.BlockSpec((blocks, rows), lambda i: (0, i + skip)),
            pl.BlockSpec((rank, cols), lambda i: (0, 0)),
        ],
        out_specs=pl.BlockSpec((rank, rows), lambda i: (0, i)),
        out_shape=jax.ShapeDtypeStruct((rank, series), F32),
        compiler_params=pltpu.CompilerParams(vmem_limit_bytes=VMEM_BYTES),
        name="factor_pull",
    )(observed, fac_t, flg_t, basis_b)


def swap(x, axis, bit):
    count = lax.axis_size(axis)
    return lax.ppermute(x, axis, [(i, i ^ bit) for i in range(count)])


def sum_over(x, axis):
    count = lax.axis_size(axis)
    if count & (count - 1):
        return lax.psum(x, axis)
    bit = 1
    while bit < count:
        x = x + swap(x, axis, bit)
        bit *= 2
    return x


def gather_over(x, axis):
    return lax.all_gather(x, axis, axis=0, tiled=False)


def shards(observed, flags, factors, basis, tcn_weights, tcn_bias, dilations):
    series, cols = observed.shape
    rank = basis.shape[0]
    time_count = lax.axis_size("tm")
    place = lax.axis_index("tm")
    fac_t, flg_t = factors.T, flags.T
    data_scale = 1.0 / math.sqrt(series * lax.axis_size("series"))
    coef = 0.1 / math.sqrt(cols * time_count)

    basis_all = gather_over(basis, "tm").transpose(1, 0, 2).reshape(rank, cols * time_count)
    sums = gather_over(sum_over(gram(observed, fac_t, flg_t, 2048), "series"), "tm")
    new_basis, basis_b = basis_steps(
        dilations, place.astype(jnp.int32).reshape(1), sums, basis_all,
        tcn_weights, tcn_bias.T, cols, data_scale,
    )

    chunks = 4
    width = series // chunks
    half = width // 2
    core = place % 2
    done = []
    for c in range(chunks):
        first = c * width
        pull = factor_pull(observed, fac_t, flg_t, basis_b, first, width, 2048) * coef
        low, high = pull[:, :half], pull[:, half:]
        own = jnp.where(core == 0, low, high)
        other = jnp.where(core == 0, high, low)
        own = (own + swap(other, "tm", 1)).astype(jnp.float16)
        both = own.astype(F32) + swap(own, "tm", 2).astype(F32)
        mine = lax.dynamic_slice_in_dim(fac_t, first + core * half, half, 1)
        new = (mine.astype(F32) - both).astype(BF16)
        theirs = swap(new, "tm", 1)
        done.append(jnp.where(core == 0, new, theirs))
        done.append(jnp.where(core == 0, theirs, new))
    return new_basis, jnp.concatenate(done, axis=1).T


def solution(mesh):
    return jax.shard_map(
        shards,
        mesh=mesh,
        in_specs=(
            P("series", "tm"),
            P("series", "tm"),
            P("series", None),
            P(None, "tm"),
            P(),
            P(),
            P(),
        ),
        out_specs=(P(None, "tm"), P("series", None)),
        check_vma=False,
    )
```

```python
import functools
import math

import jax
import jax.numpy as jnp
from jax import lax
from jax.experimental import pallas as pl
from jax.experimental.pallas import tpu as pltpu
from jax.sharding import PartitionSpec as P

BLK = 128
LANES = 128
ITERS = 3
VMEM_BYTES = 40 << 20
SMALL_BYTES = 24 << 20
PULL_ROWS = 1024
CHUNKS = (3, 5)
F32 = jnp.float32
BF16 = jnp.bfloat16


def nt_dot(a, b):
    return lax.dot_general(a, b, (((1,), (1,)), ((), ())), preferred_element_type=F32)


def tn_dot(a, b):
    return lax.dot_general(a, b, (((0,), (0,)), ((), ())), preferred_element_type=F32)


def kernel_cost(seconds):
    return pl.CostEstimate(flops=0, bytes_accessed=int(seconds * 3.69e12), transcendentals=0)


def gram_kernel(
    core_ref, obs_hbm, fac_hbm, flg_hbm, out_ref, send_hbm, obs_ref, fac_ref, flg_ref, sems,
    send_sems, *, rows
):
    series = obs_ref.shape[0]
    half = send_hbm.shape[0]
    rank, blocks = fac_ref.shape[0], flg_ref.shape[0]
    flg_copy = pltpu.make_async_copy(flg_hbm, flg_ref, sems.at[0])
    fac_copy = pltpu.make_async_copy(fac_hbm, fac_ref, sems.at[1])
    flg_copy.start()
    fac_copy.start()
    first = (1 - core_ref[0]) * half
    cuts, copies, sends = [], [], []
    for i in range(series // rows):
        at = i * rows
        at = first + at if at < half else half - first + (at - half)
        cuts.append(pl.ds(pl.multiple_of(at, rows), rows))
        copies.append(
            pltpu.make_async_copy(obs_hbm.at[cuts[i]], obs_ref.at[cuts[i]], sems.at[2 + i])
        )
        copies[i].start()
    flg_copy.wait()
    fac_copy.wait()
    for i, (cut, copy) in enumerate(zip(cuts, copies)):
        fac = fac_ref[:, cut]
        flg = flg_ref[:, cut].astype(F32).astype(BF16)
        masked = jnp.concatenate([fac * flg[b : b + 1, :] for b in range(blocks)], axis=0)
        gram_part = nt_dot(fac, masked)
        copy.wait()
        if i * rows < half:
            sends.append(
                pltpu.make_async_copy(
                    obs_ref.at[cut], send_hbm.at[pl.ds(i * rows, rows)], send_sems.at[i]
                )
            )
            sends[i].start()
        parts = []
        for b in range(0, blocks, 2):
            both = jnp.dot(
                masked[b * rank : (b + 2) * rank],
                obs_ref[cut, b * BLK : (b + 2) * BLK],
                preferred_element_type=F32,
            )
            parts += [both[:rank, :BLK], both[rank:, BLK:]]
        new = jnp.concatenate(parts + [gram_part], axis=1)
        if i == 0:
            out_ref[...] = new
        else:
            out_ref[...] += new
    for send in sends:
        send.wait()


def in_hbm(x):
    return pltpu.with_memory_space_constraint(x, pltpu.HBM)


def gram(core, observed, fac_t, flg_t, rows):
    series, cols = observed.shape
    rank, blocks = fac_t.shape[0], flg_t.shape[0]
    width = cols + blocks * rank
    half = series // 2
    hbm = pl.BlockSpec(memory_space=pltpu.HBM)
    return pl.pallas_call(
        functools.partial(gram_kernel, rows=rows),
        in_specs=[pl.BlockSpec(memory_space=pltpu.SMEM), hbm, hbm, hbm],
        out_specs=[pl.BlockSpec(memory_space=pltpu.VMEM), hbm],
        out_shape=[
            jax.ShapeDtypeStruct((rank, width), F32),
            pltpu.HBM((half, cols), BF16),
        ],
        scratch_shapes=[
            pltpu.VMEM((series, cols), BF16),
            pltpu.VMEM(fac_t.shape, BF16),
            pltpu.VMEM(flg_t.shape, jnp.int32),
            pltpu.SemaphoreType.DMA((2 + series // rows,)),
            pltpu.SemaphoreType.DMA((half // rows,)),
        ],
        compiler_params=pltpu.CompilerParams(vmem_limit_bytes=32 << 20),
        cost_estimate=kernel_cost(8e-6),
        name="gram",
    )(core, in_hbm(observed), in_hbm(fac_t), in_hbm(flg_t))


def split(x):
    high = x.astype(BF16)
    return high, (x - high.astype(F32)).astype(BF16)


def split3(x):
    high, mid = split(x)
    return high, mid, (x - high.astype(F32) - mid.astype(F32)).astype(BF16)


def later(x, steps, fill):
    lane = lax.broadcasted_iota(jnp.int32, (x.shape[0], LANES), 1)
    before = jnp.broadcast_to(fill, (x.shape[0], LANES))
    out = []
    for j in range(0, x.shape[1], LANES):
        rolled = pltpu.roll(x[:, j : j + LANES], steps, 1)
        out.append(jnp.where(lane < steps, before, rolled))
        before = rolled
    return jnp.concatenate(out, axis=1)


def earlier(x, steps):
    lane = lax.broadcasted_iota(jnp.int32, (x.shape[0], LANES), 1)
    rolled = [
        pltpu.roll(x[:, j : j + LANES], LANES - steps, 1) for j in range(0, x.shape[1], LANES)
    ]
    rolled.append(jnp.zeros((x.shape[0], LANES), F32))
    out = [jnp.where(lane < LANES - steps, a, b) for a, b in zip(rolled[:-1], rolled[1:])]
    return jnp.concatenate(out, axis=1)


def taps(first, second):
    fh, fl = split(first)
    sh, sl = split(second)
    zero = jnp.zeros_like(fh)
    top = jnp.concatenate([fh, sh, fh, sh], axis=1)
    bottom = jnp.concatenate([fl, sl, zero, zero], axis=1)
    return jnp.concatenate([top, bottom], axis=0)


def pair_dot(weights, a, b):
    ah, al = split(a)
    bh, bl = split(b)
    both = jnp.dot(
        weights, jnp.concatenate([ah, bh, al, bl], axis=0), preferred_element_type=F32
    )
    rank = a.shape[0]
    return both[:rank] + both[rank:]


def column(row):
    shape = (row.shape[1], row.shape[1])
    same = lax.broadcasted_iota(jnp.int32, shape, 0) == lax.broadcasted_iota(jnp.int32, shape, 1)
    return jnp.sum(jnp.where(same, jnp.broadcast_to(row, shape), 0.0), axis=1, keepdims=True)


def reg_gradient(x, dil_ref, w_ref, bias_ref):
    d0, d1 = dil_ref[0], dil_ref[1]
    b0, b1 = column(bias_ref[0:1, :]), column(bias_ref[1:2, :])
    w = [w_ref[i] for i in range(4)]
    z = later(x, 1, 0.0)
    pre = pair_dot(taps(w[0], w[1]), later(z, d0, 0.0), z) + b0
    hidden = jnp.maximum(pre, 0.0)
    shown = later(hidden, d1, jnp.maximum(b0, 0.0))
    error = 0.1 * (x - z - pair_dot(taps(w[2], w[3]), shown, hidden) - b1)
    pull = -pair_dot(taps(w[2].T, w[3].T), earlier(error, d1), error)
    pull = jnp.where(pre > 0.0, pull, 0.0)
    back = pair_dot(taps(w[0].T, w[1].T), earlier(pull, d0), pull)
    return error + earlier(back - error, 1)


def steps_kernel(
    dil_ref, place_ref, w_hbm, bias_hbm, *refs, slabs, data_scale, entries, series
):
    sums_hbm, basis_hbm = refs[:slabs], refs[slabs : 2 * slabs]
    own_hbm, sib_hbm, fac_hbm, own_flg_hbm, sib_flg_hbm = refs[2 * slabs : 2 * slabs + 5]
    basis_out, own_b_out, sib_b_out, pull_ref = refs[2 * slabs + 5 : 2 * slabs + 9]
    x_ref, xb_ref, data_ref, sums_ref, w_ref, bias_ref, fac_ref, flg_ref, sems = refs[
        2 * slabs + 9 : -2
    ]
    pull_scratch = refs[-2:]
    core = place_ref[0] % 2
    rank, cols = basis_out.shape
    starts = [pl.multiple_of((place_ref[0] ^ m) * cols, cols) for m in range(slabs)]
    mine = pl.ds(pl.multiple_of(core * (fac_hbm.shape[1] // 2), series), series)
    pairs = [(basis_hbm[m], x_ref.at[:, pl.ds(starts[m], cols)]) for m in range(slabs)]
    pairs += [(w_hbm, w_ref), (bias_hbm, bias_ref)]
    pairs += [(sums_hbm[m], sums_ref.at[m]) for m in range(slabs)]
    late = [
        (fac_hbm.at[:, mine], fac_ref),
        (own_flg_hbm.at[:, mine], flg_ref.at[0]),
        (sib_flg_hbm.at[:, mine], flg_ref.at[1]),
    ]
    loads = [
        pltpu.make_async_copy(source, target, sems.at[i])
        for i, (source, target) in enumerate(pairs + late)
    ]
    for load in loads:
        load.start()
    copies = pull_copies(core, own_hbm, sib_hbm, pull_scratch, 0, 0, series)
    for load in loads[: len(pairs)]:
        load.wait()

    def step(i, carry):
        reg = reg_gradient(x_ref[...], dil_ref, w_ref, bias_ref)
        xb_ref[...] = x_ref[...].astype(BF16)
        for m in range(slabs):
            for b in range(0, cols // BLK, 2):
                high, mid, low = split3(sums_ref[m, :, cols + b * rank : cols + (b + 2) * rank])
                at = pl.multiple_of(starts[m] + b * BLK, 2 * BLK)
                xb = xb_ref[:, pl.ds(at, 2 * BLK)]
                zero = jnp.zeros((rank, BLK), BF16)
                right = jnp.concatenate(
                    [
                        jnp.concatenate([xb[:, :BLK], zero], axis=1),
                        jnp.concatenate([zero, xb[:, BLK:]], axis=1),
                    ],
                    axis=0,
                )
                got = jnp.dot(
                    jnp.concatenate([high, mid, low], axis=0), right, preferred_element_type=F32
                )
                got = got[:rank] + (got[rank : 2 * rank] + got[2 * rank :])
                data_ref[:, pl.ds(at, 2 * BLK)] = got - sums_ref[m, :, b * BLK : (b + 2) * BLK]
        grad = data_ref[...] * data_scale + reg
        square = jnp.sum(grad * grad)
        x_ref[...] -= grad * (0.1 * lax.rsqrt(jnp.full((1, 1), square) / entries + 1e-06))
        return carry

    lax.fori_loop(0, ITERS, step, 0)
    basis_out[...] = x_ref[:, pl.ds(starts[0], cols)]
    own_b = x_ref[:, pl.ds(starts[0], cols)].astype(BF16)
    sib_b = x_ref[:, pl.ds(starts[1], cols)].astype(BF16)
    own_b_out[...] = own_b
    sib_b_out[...] = sib_b
    for load in loads[len(pairs) :]:
        load.wait()
    pull_chunk(
        0, copies, pull_scratch, fac_ref, flg_ref.at[0], flg_ref.at[1], own_b, sib_b, pull_ref
    )


def basis_steps(
    dilations, place, weights, bias, basis, sums, observed, sibling, fac_t, flags, data_scale,
    series
):
    slabs = len(sums)
    rank, cols = basis[0].shape
    total = slabs * cols
    smem = pl.BlockSpec(memory_space=pltpu.SMEM)
    vmem = pl.BlockSpec(memory_space=pltpu.VMEM)
    operands = [weights, bias, *sums, *basis, observed, sibling, fac_t, *flags]
    kernel = functools.partial(
        steps_kernel, slabs=slabs, data_scale=data_scale, entries=float(rank * total),
        series=series,
    )
    return pl.pallas_call(
        kernel,
        in_specs=[smem, smem] + [pl.BlockSpec(memory_space=pltpu.HBM)] * len(operands),
        out_specs=[vmem] * 4,
        out_shape=[
            jax.ShapeDtypeStruct((rank, cols), F32),
            jax.ShapeDtypeStruct((rank, cols), BF16),
            jax.ShapeDtypeStruct((rank, cols), BF16),
            jax.ShapeDtypeStruct((rank, series), F32),
        ],
        scratch_shapes=[
            pltpu.VMEM((rank, total), F32),
            pltpu.VMEM((rank, total), BF16),
            pltpu.VMEM((rank, total), F32),
            pltpu.VMEM((slabs, *sums[0].shape), F32),
            pltpu.VMEM(weights.shape, F32),
            pltpu.VMEM(bias.shape, F32),
            pltpu.VMEM((rank, series), BF16),
            pltpu.VMEM((2, flags[0].shape[0], series), jnp.int32),
            pltpu.SemaphoreType.DMA((2 * slabs + 5,)),
        ]
        + pull_scratch_shapes(cols, series),
        compiler_params=pltpu.CompilerParams(vmem_limit_bytes=32 << 20),
        cost_estimate=kernel_cost(8e-6),
        name="basis_steps",
    )(dilations, place, *[in_hbm(x) for x in operands])


def pull_rows(obs, fac, flg, basis):
    pred = tn_dot(fac, basis)
    resid = (pred - obs.astype(F32)).astype(BF16)
    total = None
    for b in range(flg.shape[0]):
        block = slice(b * BLK, (b + 1) * BLK)
        term = nt_dot(basis[:, block], resid[:, block]) * flg[b : b + 1, :].astype(F32)
        total = term if total is None else total + term
    return total


def pull_scratch_shapes(cols, series):
    return [
        pltpu.VMEM((2, series, cols), BF16),
        pltpu.SemaphoreType.DMA((-(-series // PULL_ROWS), 2)),
    ]


def pull_copies(core, own_hbm, sib_hbm, scratch, first, sib_first, series):
    obs_ref, sems = scratch
    base = core * (own_hbm.shape[0] // 2) + first
    rows = min(series, PULL_ROWS)
    copies = []
    for i in range(series // rows):
        here = pl.ds(i * rows, rows)
        own = pl.ds(pl.multiple_of(base + i * rows, rows), rows)
        copies.append(
            [
                pltpu.make_async_copy(own_hbm.at[own], obs_ref.at[0, here], sems.at[i, 0]),
                pltpu.make_async_copy(
                    sib_hbm.at[pl.ds(sib_first + i * rows, rows)], obs_ref.at[1, here], sems.at[i, 1]
                ),
            ]
        )
        for copy in copies[i]:
            copy.start()
    return copies


def pull_chunk(
    base, copies, scratch, fac_ref, own_flg_ref, sib_flg_ref, own_basis, sib_basis, out_ref
):
    obs_ref = scratch[0]
    rows = out_ref.shape[1] // len(copies)
    for i, pair in enumerate(copies):
        here = pl.ds(i * rows, rows)
        own = pl.ds(pl.multiple_of(base + i * rows, rows), rows)
        fac = fac_ref[:, own]
        pair[0].wait()
        pair[1].wait()
        out_ref[:, here] = pull_rows(
            obs_ref[0, here, :], fac, own_flg_ref[:, own], own_basis
        ) + pull_rows(obs_ref[1, here, :], fac, sib_flg_ref[:, own], sib_basis)


def pull_kernel(
    core_ref, own_hbm, sib_hbm, fac_ref, own_flg_ref, sib_flg_ref, own_basis_ref, sib_basis_ref,
    out_ref, *scratch, first, sib_first
):
    copies = pull_copies(
        core_ref[0], own_hbm, sib_hbm, scratch, first, sib_first, out_ref.shape[1]
    )
    pull_chunk(
        core_ref[0] * (fac_ref.shape[1] // 2) + first, copies, scratch, fac_ref, own_flg_ref,
        sib_flg_ref, own_basis_ref[...], sib_basis_ref[...], out_ref,
    )


def factor_pull(core, observed, sibling, fac_t, flags, basis_b, first, sib_first, series):
    vmem = pl.BlockSpec(memory_space=pltpu.VMEM)
    hbm = pl.BlockSpec(memory_space=pltpu.HBM)
    return pl.pallas_call(
        functools.partial(pull_kernel, first=first, sib_first=sib_first),
        in_specs=[pl.BlockSpec(memory_space=pltpu.SMEM), hbm, hbm] + [vmem] * 5,
        out_specs=vmem,
        out_shape=jax.ShapeDtypeStruct((fac_t.shape[0], series), F32),
        scratch_shapes=pull_scratch_shapes(observed.shape[1], series),
        compiler_params=pltpu.CompilerParams(vmem_limit_bytes=24 << 20),
        cost_estimate=kernel_cost(2e-6 * series / 1024),
        name="factor_pull",
    )(core, in_hbm(observed), in_hbm(sibling), fac_t, *flags, *basis_b)


def put_kernel(core_ref, *refs, places):
    pieces, (out, sems) = refs[: 2 * len(places)], refs[-2:]
    half = out.shape[1] // 2
    copies = []
    for i, ref in enumerate(pieces):
        side = core_ref[0] if i % 2 == 0 else 1 - core_ref[0]
        at = pl.multiple_of(side * half + places[i // 2], LANES)
        copies.append(
            pltpu.make_async_copy(ref, out.at[:, pl.ds(at, ref.shape[1])], sems.at[i])
        )
        copies[-1].start()
    for copy in copies:
        copy.wait()


def put(core, pieces, places, out, shape):
    old = [] if out is None else [in_hbm(out)]
    return pl.pallas_call(
        functools.partial(put_kernel, places=places),
        in_specs=[pl.BlockSpec(memory_space=pltpu.SMEM)]
        + [pl.BlockSpec(memory_space=pltpu.VMEM)] * len(pieces)
        + [pl.BlockSpec(memory_space=pltpu.HBM)] * len(old),
        out_specs=pl.BlockSpec(memory_space=pltpu.HBM),
        out_shape=pltpu.HBM(shape, BF16),
        scratch_shapes=[pltpu.SemaphoreType.DMA((len(pieces),))],
        input_output_aliases={1 + len(pieces): 0} if old else {},
        compiler_params=pltpu.CompilerParams(vmem_limit_bytes=4 << 20),
        cost_estimate=kernel_cost(1e-6),
        name="put",
    )(core, *pieces, *old)


def swap(x, axis, bit):
    count = lax.axis_size(axis)
    return lax.ppermute(x, axis, [(i, i ^ bit) for i in range(count)])


def sum_over(x, axis):
    count = lax.axis_size(axis)
    if count & (count - 1):
        return lax.psum(x, axis)
    bit = 1
    while bit < count:
        x = x + swap(x, axis, bit)
        bit *= 2
    return x


def gather_over(x, axis):
    bit = lax.axis_size(axis) // 2
    pieces, order = [x], [0]
    while bit:
        pieces += [swap(p, axis, bit) for p in pieces]
        order += [m ^ bit for m in order]
        bit //= 2
    return [p for _, p in sorted(zip(order, pieces), key=lambda pair: pair[0])]


def after(x, *others):
    return lax.optimization_barrier((x, *others))[0]


def shards(observed, flags, factors, basis, tcn_weights, tcn_bias, dilations):
    series, cols = observed.shape
    half = series // 2
    time_count = lax.axis_size("tm")
    place = lax.axis_index("tm")
    core = (place % 2).astype(jnp.int32).reshape(1)
    fac_t, flg_t = factors.T, flags.T
    data_scale = 1.0 / math.sqrt(series * lax.axis_size("series"))
    coef = 0.1 / math.sqrt(cols * time_count)

    place = place.astype(jnp.int32).reshape(1)
    unit = half // sum(CHUNKS)

    sums, send = gram(core, observed, fac_t, flg_t, 1024)
    sibling = swap(send, "tm", 1)
    far = swap(after(basis, sums), "tm", 2)
    slabs = [basis, swap(basis, "tm", 1), far, swap(far, "tm", 1)]
    sums = sum_over(sums, "series")
    flags = (flg_t, swap(flg_t, "tm", 1))
    new_basis, own_b, sib_b, pull = basis_steps(
        dilations, place, tcn_weights, tcn_bias, slabs, gather_over(sums, "tm"),
        observed, sibling, fac_t, flags, data_scale, CHUNKS[0] * unit,
    )
    sent, arrived, pieces, firsts = [], [], [], [0]
    for c, chunk in enumerate(CHUNKS):
        first, width = firsts[c], chunk * unit
        if c > 0:
            own_b = after(own_b, *sent)
            pull = factor_pull(
                core, observed, sibling, fac_t, flags, (own_b, sib_b), first, first, width
            )
        own = (pull * coef).astype(jnp.float16)
        sent.append(after(own, *arrived) if arrived else own)
        arrived.append(swap(sent[-1], "tm", 2))
        firsts.append(first + width)
    for c, (own, got) in enumerate(zip(sent, arrived)):
        if c == len(sent) - 1:
            new_factors = put(core, pieces, firsts[:c], None, fac_t.shape)
            got = after(got, new_factors)
            pieces = []
        both = own.astype(F32) + got.astype(F32)
        mine = lax.dynamic_slice_in_dim(fac_t, core[0] * half + firsts[c], own.shape[1], 1)
        new = (mine.astype(F32) - both).astype(BF16)
        pieces += [new, swap(new, "tm", 1)]
    new_factors = put(core, pieces, firsts[-2:-1], new_factors, fac_t.shape)
    return new_basis, new_factors.T


def solution(mesh):
    return jax.shard_map(
        shards,
        mesh=mesh,
        in_specs=(
            P("series", "tm"),
            P("series", "tm"),
            P("series", None),
            P(None, "tm"),
            P(),
            P(),
            P(),
        ),
        out_specs=(P(None, "tm"), P("series", None)),
        check_vma=False,
    )
```

```python
import functools
import math

import jax
import jax.numpy as jnp
from jax import lax
from jax.experimental import pallas as pl
from jax.experimental.pallas import tpu as pltpu
from jax.sharding import PartitionSpec as P

BLK = 128
LANES = 128
ITERS = 3
VMEM_BYTES = 40 << 20
SMALL_BYTES = 24 << 20
PULL_ROWS = 1024
CHUNKS = (4, 4)
CUTS = ((2, 2), (3, 1))
F32 = jnp.float32
BF16 = jnp.bfloat16


def nt_dot(a, b):
    return lax.dot_general(a, b, (((1,), (1,)), ((), ())), preferred_element_type=F32)


def tn_dot(a, b):
    return lax.dot_general(a, b, (((0,), (0,)), ((), ())), preferred_element_type=F32)


def kernel_cost(seconds):
    return pl.CostEstimate(flops=0, bytes_accessed=int(seconds * 3.69e12), transcendentals=0)


def gram_kernel(
    core_ref, obs_hbm, fac_hbm, flg_hbm, out_ref, send_hbm, obs_ref, fac_ref, flg_ref, sems,
    send_sems, *, rows
):
    series = obs_ref.shape[0]
    half = send_hbm.shape[0]
    rank, blocks = fac_ref.shape[0], flg_ref.shape[0]
    flg_copy = pltpu.make_async_copy(flg_hbm, flg_ref, sems.at[0])
    fac_copy = pltpu.make_async_copy(fac_hbm, fac_ref, sems.at[1])
    flg_copy.start()
    fac_copy.start()
    first = (1 - core_ref[0]) * half
    cuts, copies, sends = [], [], []
    for i in range(series // rows):
        at = i * rows
        at = first + at if at < half else half - first + (at - half)
        cuts.append(pl.ds(pl.multiple_of(at, rows), rows))
        copies.append(
            pltpu.make_async_copy(obs_hbm.at[cuts[i]], obs_ref.at[cuts[i]], sems.at[2 + i])
        )
        copies[i].start()
    flg_copy.wait()
    fac_copy.wait()
    for i, (cut, copy) in enumerate(zip(cuts, copies)):
        fac = fac_ref[:, cut]
        flg = flg_ref[:, cut].astype(F32).astype(BF16)
        masked = jnp.concatenate([fac * flg[b : b + 1, :] for b in range(blocks)], axis=0)
        gram_part = nt_dot(fac, masked)
        copy.wait()
        if i * rows < half:
            sends.append(
                pltpu.make_async_copy(
                    obs_ref.at[cut], send_hbm.at[pl.ds(i * rows, rows)], send_sems.at[i]
                )
            )
            sends[i].start()
        parts = []
        for b in range(0, blocks, 2):
            both = jnp.dot(
                masked[b * rank : (b + 2) * rank],
                obs_ref[cut, b * BLK : (b + 2) * BLK],
                preferred_element_type=F32,
            )
            parts += [both[:rank, :BLK], both[rank:, BLK:]]
        new = jnp.concatenate(parts + [gram_part], axis=1)
        if i == 0:
            out_ref[...] = new
        else:
            out_ref[...] += new
    for send in sends:
        send.wait()


def in_hbm(x):
    return pltpu.with_memory_space_constraint(x, pltpu.HBM)


def gram(core, observed, fac_t, flg_t, rows):
    series, cols = observed.shape
    rank, blocks = fac_t.shape[0], flg_t.shape[0]
    width = cols + blocks * rank
    half = series // 2
    hbm = pl.BlockSpec(memory_space=pltpu.HBM)
    return pl.pallas_call(
        functools.partial(gram_kernel, rows=rows),
        in_specs=[pl.BlockSpec(memory_space=pltpu.SMEM), hbm, hbm, hbm],
        out_specs=[pl.BlockSpec(memory_space=pltpu.VMEM), hbm],
        out_shape=[
            jax.ShapeDtypeStruct((rank, width), F32),
            pltpu.HBM((half, cols), BF16),
        ],
        scratch_shapes=[
            pltpu.VMEM((series, cols), BF16),
            pltpu.VMEM(fac_t.shape, BF16),
            pltpu.VMEM(flg_t.shape, jnp.int32),
            pltpu.SemaphoreType.DMA((2 + series // rows,)),
            pltpu.SemaphoreType.DMA((half // rows,)),
        ],
        compiler_params=pltpu.CompilerParams(vmem_limit_bytes=32 << 20),
        cost_estimate=kernel_cost(8e-6),
        name="gram",
    )(core, in_hbm(observed), in_hbm(fac_t), in_hbm(flg_t))


def split(x):
    high = x.astype(BF16)
    return high, (x - high.astype(F32)).astype(BF16)


def split3(x):
    high, mid = split(x)
    return high, mid, (x - high.astype(F32) - mid.astype(F32)).astype(BF16)


def later(x, steps, fill):
    lane = lax.broadcasted_iota(jnp.int32, (x.shape[0], LANES), 1)
    before = jnp.broadcast_to(fill, (x.shape[0], LANES))
    out = []
    for j in range(0, x.shape[1], LANES):
        rolled = pltpu.roll(x[:, j : j + LANES], steps, 1)
        out.append(jnp.where(lane < steps, before, rolled))
        before = rolled
    return jnp.concatenate(out, axis=1)


def earlier(x, steps):
    lane = lax.broadcasted_iota(jnp.int32, (x.shape[0], LANES), 1)
    rolled = [
        pltpu.roll(x[:, j : j + LANES], LANES - steps, 1) for j in range(0, x.shape[1], LANES)
    ]
    rolled.append(jnp.zeros((x.shape[0], LANES), F32))
    out = [jnp.where(lane < LANES - steps, a, b) for a, b in zip(rolled[:-1], rolled[1:])]
    return jnp.concatenate(out, axis=1)


def taps(first, second):
    fh, fl = split(first)
    sh, sl = split(second)
    zero = jnp.zeros_like(fh)
    top = jnp.concatenate([fh, sh, fh, sh], axis=1)
    bottom = jnp.concatenate([fl, sl, zero, zero], axis=1)
    return jnp.concatenate([top, bottom], axis=0)


def pair_dot(weights, a, b):
    ah, al = split(a)
    bh, bl = split(b)
    both = jnp.dot(
        weights, jnp.concatenate([ah, bh, al, bl], axis=0), preferred_element_type=F32
    )
    rank = a.shape[0]
    return both[:rank] + both[rank:]


def column(row):
    shape = (row.shape[1], row.shape[1])
    same = lax.broadcasted_iota(jnp.int32, shape, 0) == lax.broadcasted_iota(jnp.int32, shape, 1)
    return jnp.sum(jnp.where(same, jnp.broadcast_to(row, shape), 0.0), axis=1, keepdims=True)


def reg_gradient(x, dil_ref, w_ref, bias_ref):
    d0, d1 = dil_ref[0], dil_ref[1]
    b0, b1 = column(bias_ref[0:1, :]), column(bias_ref[1:2, :])
    w = [w_ref[i] for i in range(4)]
    z = later(x, 1, 0.0)
    pre = pair_dot(taps(w[0], w[1]), later(z, d0, 0.0), z) + b0
    hidden = jnp.maximum(pre, 0.0)
    shown = later(hidden, d1, jnp.maximum(b0, 0.0))
    error = 0.1 * (x - z - pair_dot(taps(w[2], w[3]), shown, hidden) - b1)
    pull = -pair_dot(taps(w[2].T, w[3].T), earlier(error, d1), error)
    pull = jnp.where(pre > 0.0, pull, 0.0)
    back = pair_dot(taps(w[0].T, w[1].T), earlier(pull, d0), pull)
    return error + earlier(back - error, 1)


def network_kernel(dil_ref, place_ref, w_hbm, bias_hbm, *refs, slabs):
    basis_hbm, (x_hbm, reg_hbm, x_ref, reg_ref, w_ref, bias_ref, sems) = refs[:slabs], refs[slabs:]
    cols = basis_hbm[0].shape[1]
    pairs = [(w_hbm, w_ref), (bias_hbm, bias_ref)]
    for m in range(slabs):
        start = pl.multiple_of((place_ref[0] ^ m) * cols, cols)
        pairs.append((basis_hbm[m], x_ref.at[:, pl.ds(start, cols)]))
    loads = [
        pltpu.make_async_copy(source, target, sems.at[i])
        for i, (source, target) in enumerate(pairs)
    ]
    for load in loads:
        load.start()
    for load in loads:
        load.wait()
    x_store = pltpu.make_async_copy(x_ref, x_hbm, sems.at[slabs + 2])
    reg_store = pltpu.make_async_copy(reg_ref, reg_hbm, sems.at[slabs + 3])
    x_store.start()
    reg_ref[...] = reg_gradient(x_ref[...], dil_ref, w_ref, bias_ref)
    reg_store.start()
    x_store.wait()
    reg_store.wait()


def network_start(dilations, place, weights, bias, basis):
    slabs = len(basis)
    rank, cols = basis[0].shape
    smem = pl.BlockSpec(memory_space=pltpu.SMEM)
    hbm = pl.BlockSpec(memory_space=pltpu.HBM)
    whole = (rank, slabs * cols)
    return pl.pallas_call(
        functools.partial(network_kernel, slabs=slabs),
        in_specs=[smem, smem] + [hbm] * (2 + slabs),
        out_specs=[hbm, hbm],
        out_shape=[pltpu.HBM(whole, F32), pltpu.HBM(whole, F32)],
        scratch_shapes=[
            pltpu.VMEM(whole, F32),
            pltpu.VMEM(whole, F32),
            pltpu.VMEM(weights.shape, F32),
            pltpu.VMEM(bias.shape, F32),
            pltpu.SemaphoreType.DMA((slabs + 4,)),
        ],
        compiler_params=pltpu.CompilerParams(vmem_limit_bytes=16 << 20),
        cost_estimate=kernel_cost(3e-6),
        name="network_start",
    )(dilations, place, *[in_hbm(x) for x in (weights, bias, *basis)])


def steps_kernel(
    dil_ref, place_ref, w_hbm, bias_hbm, *refs, slabs, data_scale, entries, series
):
    sums_hbm, x_hbm, reg_hbm = refs[:slabs], refs[slabs], refs[slabs + 1]
    own_hbm, sib_hbm, fac_hbm, own_flg_hbm, sib_flg_hbm = refs[slabs + 2 : slabs + 7]
    basis_out, own_b_out, sib_b_out, pull_ref = refs[slabs + 7 : slabs + 11]
    x_ref, reg_ref, xb_ref, data_ref, sums_ref, w_ref, bias_ref, fac_ref, flg_ref, sems = refs[
        slabs + 11 : -2
    ]
    pull_scratch = refs[-2:]
    core = place_ref[0] % 2
    rank, cols = basis_out.shape
    starts = [pl.multiple_of((place_ref[0] ^ m) * cols, cols) for m in range(slabs)]
    mine = pl.ds(pl.multiple_of(core * (fac_hbm.shape[1] // 2), series), series)
    pairs = [(x_hbm, x_ref)] + [(sums_hbm[m], sums_ref.at[m]) for m in range(slabs)]
    pairs += [(reg_hbm, reg_ref), (w_hbm, w_ref), (bias_hbm, bias_ref)]
    late = [
        (fac_hbm.at[:, mine], fac_ref),
        (own_flg_hbm.at[:, mine], flg_ref.at[0]),
        (sib_flg_hbm.at[:, mine], flg_ref.at[1]),
    ]
    loads = [
        pltpu.make_async_copy(source, target, sems.at[i])
        for i, (source, target) in enumerate(pairs + late)
    ]
    for load in loads:
        load.start()
    tiles = pull_tiles(series, True)
    copies = pull_copies(core, own_hbm, sib_hbm, pull_scratch, 0, tiles)
    for load in loads[: len(pairs)]:
        load.wait()

    def step():
        xb_ref[...] = x_ref[...].astype(BF16)
        for m in range(slabs):
            for b in range(0, cols // BLK, 2):
                high, mid, low = split3(sums_ref[m, :, cols + b * rank : cols + (b + 2) * rank])
                at = pl.multiple_of(starts[m] + b * BLK, 2 * BLK)
                xb = xb_ref[:, pl.ds(at, 2 * BLK)]
                zero = jnp.zeros((rank, BLK), BF16)
                right = jnp.concatenate(
                    [
                        jnp.concatenate([xb[:, :BLK], zero], axis=1),
                        jnp.concatenate([zero, xb[:, BLK:]], axis=1),
                    ],
                    axis=0,
                )
                got = jnp.dot(
                    jnp.concatenate([high, mid, low], axis=0), right, preferred_element_type=F32
                )
                got = got[:rank] + (got[rank : 2 * rank] + got[2 * rank :])
                data_ref[:, pl.ds(at, 2 * BLK)] = got - sums_ref[m, :, b * BLK : (b + 2) * BLK]
        grad = data_ref[...] * data_scale + reg_ref[...]
        square = jnp.sum(grad * grad)
        x_ref[...] -= grad * (0.1 * lax.rsqrt(jnp.full((1, 1), square) / entries + 1e-06))

    def body(i, carry):
        reg_ref[...] = reg_gradient(x_ref[...], dil_ref, w_ref, bias_ref)
        step()
        return carry

    step()
    lax.fori_loop(1, ITERS, body, 0)
    basis_out[...] = x_ref[:, pl.ds(starts[0], cols)]
    own_b = x_ref[:, pl.ds(starts[0], cols)].astype(BF16)
    sib_b = x_ref[:, pl.ds(starts[1], cols)].astype(BF16)
    own_b_out[...] = own_b
    sib_b_out[...] = sib_b
    for load in loads[len(pairs) :]:
        load.wait()
    pull_chunk(
        0, tiles, copies, pull_scratch, fac_ref, flg_ref.at[0], flg_ref.at[1], own_b, sib_b,
        pull_ref,
    )


def basis_steps(
    dilations, place, weights, bias, start, sums, observed, sibling, fac_t, flags, data_scale,
    series
):
    slabs = len(sums)
    rank, total = start[0].shape
    cols = total // slabs
    smem = pl.BlockSpec(memory_space=pltpu.SMEM)
    vmem = pl.BlockSpec(memory_space=pltpu.VMEM)
    operands = [weights, bias, *sums, *start, observed, sibling, fac_t, *flags]
    kernel = functools.partial(
        steps_kernel, slabs=slabs, data_scale=data_scale, entries=float(rank * total),
        series=series,
    )
    return pl.pallas_call(
        kernel,
        in_specs=[smem, smem] + [pl.BlockSpec(memory_space=pltpu.HBM)] * len(operands),
        out_specs=[vmem] * 4,
        out_shape=[
            jax.ShapeDtypeStruct((rank, cols), F32),
            jax.ShapeDtypeStruct((rank, cols), BF16),
            jax.ShapeDtypeStruct((rank, cols), BF16),
            jax.ShapeDtypeStruct((rank, series), F32),
        ],
        scratch_shapes=[
            pltpu.VMEM((rank, total), F32),
            pltpu.VMEM((rank, total), F32),
            pltpu.VMEM((rank, total), BF16),
            pltpu.VMEM((rank, total), F32),
            pltpu.VMEM((slabs, *sums[0].shape), F32),
            pltpu.VMEM(weights.shape, F32),
            pltpu.VMEM(bias.shape, F32),
            pltpu.VMEM((rank, series), BF16),
            pltpu.VMEM((2, flags[0].shape[0], series), jnp.int32),
            pltpu.SemaphoreType.DMA((slabs + 7,)),
        ]
        + pull_scratch_shapes(cols, series, pull_tiles(series, True)),
        compiler_params=pltpu.CompilerParams(vmem_limit_bytes=32 << 20),
        cost_estimate=kernel_cost(8e-6),
        name="basis_steps",
    )(dilations, place, *[in_hbm(x) for x in operands])


def pull_rows(obs, fac, flg, basis):
    pred = tn_dot(fac, basis)
    resid = (pred - obs.astype(F32)).astype(BF16)
    total = None
    for b in range(flg.shape[0]):
        block = slice(b * BLK, (b + 1) * BLK)
        term = nt_dot(basis[:, block], resid[:, block]) * flg[b : b + 1, :].astype(F32)
        total = term if total is None else total + term
    return total


def pull_tiles(series, ready):
    first = series if ready or series <= PULL_ROWS else PULL_ROWS
    tiles, at = [(0, first)], first
    while at < series:
        tiles.append((at, min(3 * PULL_ROWS, series - at)))
        at += tiles[-1][1]
    return tiles


def pull_scratch_shapes(cols, series, tiles):
    return [
        pltpu.VMEM((2, series, cols), BF16),
        pltpu.SemaphoreType.DMA((len(tiles), 2)),
    ]


def pull_copies(core, own_hbm, sib_hbm, scratch, first, tiles):
    obs_ref, sems = scratch
    base = core * (own_hbm.shape[0] // 2) + first
    copies = []
    for i, (at, rows) in enumerate(tiles):
        here = pl.ds(at, rows)
        own = pl.ds(pl.multiple_of(base + at, PULL_ROWS), rows)
        copies.append(
            [
                pltpu.make_async_copy(own_hbm.at[own], obs_ref.at[0, here], sems.at[i, 0]),
                pltpu.make_async_copy(
                    sib_hbm.at[pl.ds(first + at, rows)], obs_ref.at[1, here], sems.at[i, 1]
                ),
            ]
        )
        for copy in copies[i]:
            copy.start()
    return copies


def pull_chunk(
    base, tiles, copies, scratch, fac_ref, own_flg_ref, sib_flg_ref, own_basis, sib_basis, out_ref
):
    obs_ref = scratch[0]
    for (first, height), pair in zip(tiles, copies):
        pair[0].wait()
        pair[1].wait()
        for at in range(first, first + height, 2 * PULL_ROWS):
            rows = min(2 * PULL_ROWS, first + height - at)
            here = pl.ds(at, rows)
            own = pl.ds(pl.multiple_of(base + at, PULL_ROWS), rows)
            fac = fac_ref[:, own]
            out_ref[:, here] = pull_rows(
                obs_ref[0, here, :], fac, own_flg_ref[:, own], own_basis
            ) + pull_rows(obs_ref[1, here, :], fac, sib_flg_ref[:, own], sib_basis)


def pull_kernel(
    core_ref, own_hbm, sib_hbm, fac_ref, own_flg_ref, sib_flg_ref, own_basis_ref, sib_basis_ref,
    out_ref, *scratch, first, tiles
):
    copies = pull_copies(core_ref[0], own_hbm, sib_hbm, scratch, first, tiles)
    pull_chunk(
        core_ref[0] * (fac_ref.shape[1] // 2) + first, tiles, copies, scratch, fac_ref, own_flg_ref,
        sib_flg_ref, own_basis_ref[...], sib_basis_ref[...], out_ref,
    )


def factor_pull(core, observed, sibling, fac_t, flags, basis_b, first, series):
    vmem = pl.BlockSpec(memory_space=pltpu.VMEM)
    hbm = pl.BlockSpec(memory_space=pltpu.HBM)
    tiles = pull_tiles(series, False)
    return pl.pallas_call(
        functools.partial(pull_kernel, first=first, tiles=tiles),
        in_specs=[pl.BlockSpec(memory_space=pltpu.SMEM), hbm, hbm] + [vmem] * 5,
        out_specs=vmem,
        out_shape=jax.ShapeDtypeStruct((fac_t.shape[0], series), F32),
        scratch_shapes=pull_scratch_shapes(observed.shape[1], series, tiles),
        compiler_params=pltpu.CompilerParams(vmem_limit_bytes=24 << 20),
        cost_estimate=kernel_cost(2e-6 * series / 1024),
        name="factor_pull",
    )(core, in_hbm(observed), in_hbm(sibling), fac_t, *flags, *basis_b)


def put_kernel(core_ref, *refs, places):
    pieces, (out, sems) = refs[: 2 * len(places)], refs[-2:]
    half = out.shape[1] // 2
    copies = []
    for i, ref in enumerate(pieces):
        side = core_ref[0] if i % 2 == 0 else 1 - core_ref[0]
        at = pl.multiple_of(side * half + places[i // 2], LANES)
        copies.append(
            pltpu.make_async_copy(ref, out.at[:, pl.ds(at, ref.shape[1])], sems.at[i])
        )
        copies[-1].start()
    for copy in copies:
        copy.wait()


def put(core, pieces, places, out, shape):
    old = [] if out is None else [in_hbm(out)]
    return pl.pallas_call(
        functools.partial(put_kernel, places=places),
        in_specs=[pl.BlockSpec(memory_space=pltpu.SMEM)]
        + [pl.BlockSpec(memory_space=pltpu.VMEM)] * len(pieces)
        + [pl.BlockSpec(memory_space=pltpu.HBM)] * len(old),
        out_specs=pl.BlockSpec(memory_space=pltpu.HBM),
        out_shape=pltpu.HBM(shape, BF16),
        scratch_shapes=[pltpu.SemaphoreType.DMA((len(pieces),))],
        input_output_aliases={1 + len(pieces): 0} if old else {},
        compiler_params=pltpu.CompilerParams(vmem_limit_bytes=4 << 20),
        cost_estimate=kernel_cost(1e-6),
        name="put",
    )(core, *pieces, *old)


def swap(x, axis, bit):
    count = lax.axis_size(axis)
    return lax.ppermute(x, axis, [(i, i ^ bit) for i in range(count)])


def sum_over(x, axis, beside):
    count = lax.axis_size(axis)
    if count & (count - 1):
        return lax.psum(x, axis)
    bit = 1
    while bit < count:
        other = swap(x, axis, bit)
        if beside:
            done = beside.pop(0)(x)
            x = after(x + other, *done)
        else:
            x = x + other
        bit *= 2
    return x


def after(x, *others):
    return lax.optimization_barrier((x, *others))[0]


def shards(observed, flags, factors, basis, tcn_weights, tcn_bias, dilations):
    series, cols = observed.shape
    half = series // 2
    time_count = lax.axis_size("tm")
    place = lax.axis_index("tm")
    core = (place % 2).astype(jnp.int32).reshape(1)
    fac_t, flg_t = factors.T, flags.T
    data_scale = 1.0 / math.sqrt(series * lax.axis_size("series"))
    coef = 0.1 / math.sqrt(cols * time_count)

    place = place.astype(jnp.int32).reshape(1)
    unit = half // sum(CHUNKS)

    sums, send = gram(core, observed, fac_t, flg_t, 1024)
    sibling = swap(send, "tm", 1)
    slabs = {0: basis}

    def beside_1(now):
        slabs[2] = swap(after(basis, now), "tm", 2)
        return [slabs[2]]

    def beside_2(now):
        return []

    def beside_3(now):
        slabs[1] = swap(after(basis, now), "tm", 1)
        slabs[3] = swap(after(slabs[2], now), "tm", 1)
        slabs["flags"] = swap(after(flg_t, now), "tm", 1)
        return [slabs[1], slabs[3]]

    beside = [beside_1, beside_2, beside_3]
    sums = sum_over(sums, "series", beside)
    for work in beside:
        work(sums)
    flags = (flg_t, slabs["flags"])
    start = network_start(
        dilations, after(place, sums), tcn_weights, tcn_bias, [slabs[m] for m in range(time_count)]
    )
    far = after(swap(sums, "tm", 2), start[1])
    sums = [sums, swap(sums, "tm", 1), far, swap(far, "tm", 1)]
    new_basis, own_b, sib_b, pull = basis_steps(
        dilations, place, tcn_weights, tcn_bias, start, sums,
        observed, sibling, fac_t, flags, data_scale, CHUNKS[0] * unit,
    )
    sent, arrived, pieces, firsts = [], [], [], []
    first = 0
    for c, chunk in enumerate(CHUNKS):
        width = chunk * unit
        if c > 0:
            own_b = after(own_b, *sent)
            pull = factor_pull(
                core, observed, sibling, fac_t, flags, (own_b, sib_b), first, width
            )
        own = (pull * coef).astype(jnp.float16)
        at = 0
        for cut in CUTS[c]:
            piece = own[:, at * unit : (at + cut) * unit]
            if c > 0:
                piece = after(piece, arrived[0])
            sent.append(piece)
            arrived.append(swap(piece, "tm", 2))
            firsts.append(first + at * unit)
            at += cut
        first += width
    early = len(CUTS[0])
    for c, (own, got) in enumerate(zip(sent, arrived)):
        if c < early:
            got = after(got, *sent[early:])
        if c == early:
            new_factors = put(core, pieces, firsts[:early], None, fac_t.shape)
            pieces = []
        if c >= early:
            got = after(got, new_factors)
        both = own.astype(F32) + got.astype(F32)
        mine = lax.dynamic_slice_in_dim(fac_t, core[0] * half + firsts[c], own.shape[1], 1)
        new = (mine.astype(F32) - both).astype(BF16)
        pieces += [new, swap(new, "tm", 1)]
    new_factors = put(core, pieces, firsts[early:], new_factors, fac_t.shape)
    return new_basis, new_factors.T


def solution(mesh):
    return jax.shard_map(
        shards,
        mesh=mesh,
        in_specs=(
            P("series", "tm"),
            P("series", "tm"),
            P("series", None),
            P(None, "tm"),
            P(),
            P(),
            P(),
        ),
        out_specs=(P(None, "tm"), P("series", None)),
        check_vma=False,
    )
```

```python
import functools
import math

import jax
import jax.numpy as jnp
from jax import lax
from jax.experimental import pallas as pl
from jax.experimental.pallas import tpu as pltpu
from jax.sharding import PartitionSpec as P

BLK = 128
LANES = 128
ITERS = 3
VMEM_BYTES = 40 << 20
SMALL_BYTES = 24 << 20
PULL_ROWS = 1024
CHUNKS = (4, 4)
CUTS = ((2, 2), (3, 1))
F32 = jnp.float32
BF16 = jnp.bfloat16


def nt_dot(a, b):
    return lax.dot_general(a, b, (((1,), (1,)), ((), ())), preferred_element_type=F32)


def tn_dot(a, b):
    return lax.dot_general(a, b, (((0,), (0,)), ((), ())), preferred_element_type=F32)


def kernel_cost(seconds):
    return pl.CostEstimate(flops=0, bytes_accessed=int(seconds * 3.69e12), transcendentals=0)


def gram_kernel(
    obs_hbm, fac_hbm, flg_hbm, out_ref, obs_ref, fac_ref, flg_ref, sems, *, rows
):
    series = obs_ref.shape[0]
    rank, blocks = fac_ref.shape[0], flg_ref.shape[0]
    flg_copy = pltpu.make_async_copy(flg_hbm, flg_ref, sems.at[0])
    flg_copy.start()
    steps = series // rows
    fac_copies, copies = [], []
    for i in range(steps):
        if i % (steps // 2) == 0:
            cut = pl.ds(i * rows, series // 2)
            fac_copies.append(
                pltpu.make_async_copy(
                    fac_hbm.at[:, cut], fac_ref.at[:, cut], sems.at[1 + len(fac_copies)]
                )
            )
            fac_copies[-1].start()
        cut = pl.ds(i * rows, rows)
        copies.append(pltpu.make_async_copy(obs_hbm.at[cut], obs_ref.at[cut], sems.at[3 + i]))
        copies[i].start()
    flg_copy.wait()
    for i, copy in enumerate(copies):
        if i % (steps // 2) == 0:
            fac_copies[i // (steps // 2)].wait()
        cut = pl.ds(i * rows, rows)
        fac = fac_ref[:, cut]
        flg = flg_ref[:, cut].astype(F32).astype(BF16)
        masked = jnp.concatenate([fac * flg[b : b + 1, :] for b in range(blocks)], axis=0)
        gram_part = nt_dot(fac, masked)
        copy.wait()
        parts = []
        for b in range(0, blocks, 2):
            both = jnp.dot(
                masked[b * rank : (b + 2) * rank],
                obs_ref[cut, b * BLK : (b + 2) * BLK],
                preferred_element_type=F32,
            )
            parts += [both[:rank, :BLK], both[rank:, BLK:]]
        new = jnp.concatenate(parts + [gram_part], axis=1)
        if i == 0:
            out_ref[...] = new
        else:
            out_ref[...] += new


def part_kernel(core_ref, obs_hbm, out_hbm, part_ref, sems, *, first, pieces):
    rows = out_hbm.shape[0] // pieces
    base = (1 - core_ref[0]) * (obs_hbm.shape[0] // 2) + first
    loads, stores = [], []
    for i in range(pieces):
        here = pl.ds(i * rows, rows)
        there = pl.ds(pl.multiple_of(base + i * rows, rows), rows)
        loads.append(pltpu.make_async_copy(obs_hbm.at[there], part_ref.at[here], sems.at[i, 0]))
        stores.append(pltpu.make_async_copy(part_ref.at[here], out_hbm.at[here], sems.at[i, 1]))
    for load in loads:
        load.start()
    for load, store in zip(loads, stores):
        load.wait()
        store.start()
    for store in stores:
        store.wait()


def other_part(core, observed, first, rows):
    hbm = pl.BlockSpec(memory_space=pltpu.HBM)
    pieces = 8
    return pl.pallas_call(
        functools.partial(part_kernel, first=first, pieces=pieces),
        in_specs=[pl.BlockSpec(memory_space=pltpu.SMEM), hbm],
        out_specs=hbm,
        out_shape=pltpu.HBM((rows, observed.shape[1]), observed.dtype),
        scratch_shapes=[
            pltpu.VMEM((rows, observed.shape[1]), observed.dtype),
            pltpu.SemaphoreType.DMA((pieces, 2)),
        ],
        compiler_params=pltpu.CompilerParams(vmem_limit_bytes=16 << 20),
        cost_estimate=kernel_cost(3e-6),
        name="other_part",
    )(core, in_hbm(observed))


def in_hbm(x):
    return pltpu.with_memory_space_constraint(x, pltpu.HBM)


def gram(observed, fac_t, flg_t, rows):
    series, cols = observed.shape
    rank, blocks = fac_t.shape[0], flg_t.shape[0]
    width = cols + blocks * rank
    hbm = pl.BlockSpec(memory_space=pltpu.HBM)
    return pl.pallas_call(
        functools.partial(gram_kernel, rows=rows),
        in_specs=[hbm, hbm, hbm],
        out_specs=pl.BlockSpec(memory_space=pltpu.VMEM),
        out_shape=jax.ShapeDtypeStruct((rank, width), F32),
        scratch_shapes=[
            pltpu.VMEM((series, cols), BF16),
            pltpu.VMEM(fac_t.shape, BF16),
            pltpu.VMEM(flg_t.shape, jnp.int32),
            pltpu.SemaphoreType.DMA((3 + series // rows,)),
        ],
        compiler_params=pltpu.CompilerParams(vmem_limit_bytes=32 << 20),
        cost_estimate=kernel_cost(8e-6),
        name="gram",
    )(in_hbm(observed), in_hbm(fac_t), in_hbm(flg_t))


def split(x):
    high = x.astype(BF16)
    return high, (x - high.astype(F32)).astype(BF16)


def split3(x):
    high, mid = split(x)
    return high, mid, (x - high.astype(F32) - mid.astype(F32)).astype(BF16)


def later(x, steps, fill):
    lane = lax.broadcasted_iota(jnp.int32, (x.shape[0], LANES), 1)
    before = jnp.broadcast_to(fill, (x.shape[0], LANES))
    out = []
    for j in range(0, x.shape[1], LANES):
        rolled = pltpu.roll(x[:, j : j + LANES], steps, 1)
        out.append(jnp.where(lane < steps, before, rolled))
        before = rolled
    return jnp.concatenate(out, axis=1)


def earlier(x, steps):
    lane = lax.broadcasted_iota(jnp.int32, (x.shape[0], LANES), 1)
    rolled = [
        pltpu.roll(x[:, j : j + LANES], LANES - steps, 1) for j in range(0, x.shape[1], LANES)
    ]
    rolled.append(jnp.zeros((x.shape[0], LANES), F32))
    out = [jnp.where(lane < LANES - steps, a, b) for a, b in zip(rolled[:-1], rolled[1:])]
    return jnp.concatenate(out, axis=1)


def taps(first, second):
    fh, fl = split(first)
    sh, sl = split(second)
    zero = jnp.zeros_like(fh)
    top = jnp.concatenate([fh, sh, fh, sh], axis=1)
    bottom = jnp.concatenate([fl, sl, zero, zero], axis=1)
    return jnp.concatenate([top, bottom], axis=0)


def pair_dot(weights, a, b):
    ah, al = split(a)
    bh, bl = split(b)
    both = jnp.dot(
        weights, jnp.concatenate([ah, bh, al, bl], axis=0), preferred_element_type=F32
    )
    rank = a.shape[0]
    return both[:rank] + both[rank:]


def column(row):
    shape = (row.shape[1], row.shape[1])
    same = lax.broadcasted_iota(jnp.int32, shape, 0) == lax.broadcasted_iota(jnp.int32, shape, 1)
    return jnp.sum(jnp.where(same, jnp.broadcast_to(row, shape), 0.0), axis=1, keepdims=True)


def reg_gradient(x, dil_ref, w_ref, bias_ref):
    d0, d1 = dil_ref[0], dil_ref[1]
    b0, b1 = column(bias_ref[0:1, :]), column(bias_ref[1:2, :])
    w = [w_ref[i] for i in range(4)]
    z = later(x, 1, 0.0)
    pre = pair_dot(taps(w[0], w[1]), later(z, d0, 0.0), z) + b0
    hidden = jnp.maximum(pre, 0.0)
    shown = later(hidden, d1, jnp.maximum(b0, 0.0))
    error = 0.1 * (x - z - pair_dot(taps(w[2], w[3]), shown, hidden) - b1)
    pull = -pair_dot(taps(w[2].T, w[3].T), earlier(error, d1), error)
    pull = jnp.where(pre > 0.0, pull, 0.0)
    back = pair_dot(taps(w[0].T, w[1].T), earlier(pull, d0), pull)
    return error + earlier(back - error, 1)


def network_kernel(dil_ref, place_ref, w_hbm, bias_hbm, *refs, slabs):
    basis_hbm, (x_hbm, reg_hbm, x_ref, reg_ref, w_ref, bias_ref, sems) = refs[:slabs], refs[slabs:]
    cols = basis_hbm[0].shape[1]
    pairs = [(w_hbm, w_ref), (bias_hbm, bias_ref)]
    for m in range(slabs):
        start = pl.multiple_of((place_ref[0] ^ m) * cols, cols)
        pairs.append((basis_hbm[m], x_ref.at[:, pl.ds(start, cols)]))
    loads = [
        pltpu.make_async_copy(source, target, sems.at[i])
        for i, (source, target) in enumerate(pairs)
    ]
    for load in loads:
        load.start()
    for load in loads:
        load.wait()
    x_store = pltpu.make_async_copy(x_ref, x_hbm, sems.at[slabs + 2])
    reg_store = pltpu.make_async_copy(reg_ref, reg_hbm, sems.at[slabs + 3])
    x_store.start()
    reg_ref[...] = reg_gradient(x_ref[...], dil_ref, w_ref, bias_ref)
    reg_store.start()
    x_store.wait()
    reg_store.wait()


def network_start(dilations, place, weights, bias, basis):
    slabs = len(basis)
    rank, cols = basis[0].shape
    smem = pl.BlockSpec(memory_space=pltpu.SMEM)
    hbm = pl.BlockSpec(memory_space=pltpu.HBM)
    whole = (rank, slabs * cols)
    return pl.pallas_call(
        functools.partial(network_kernel, slabs=slabs),
        in_specs=[smem, smem] + [hbm] * (2 + slabs),
        out_specs=[hbm, hbm],
        out_shape=[pltpu.HBM(whole, F32), pltpu.HBM(whole, F32)],
        scratch_shapes=[
            pltpu.VMEM(whole, F32),
            pltpu.VMEM(whole, F32),
            pltpu.VMEM(weights.shape, F32),
            pltpu.VMEM(bias.shape, F32),
            pltpu.SemaphoreType.DMA((slabs + 4,)),
        ],
        compiler_params=pltpu.CompilerParams(vmem_limit_bytes=16 << 20),
        cost_estimate=kernel_cost(3e-6),
        name="network_start",
    )(dilations, place, *[in_hbm(x) for x in (weights, bias, *basis)])


def steps_kernel(
    dil_ref, place_ref, last_ref, w_hbm, bias_hbm, *refs, slabs, data_scale, entries, series
):
    sums_hbm, refs = refs[: slabs - 1], refs[slabs - 1 :]
    x_hbm, reg_hbm, own_hbm, sib_hbm, fac_hbm, own_flg_hbm, sib_flg_hbm = refs[:7]
    basis_out, own_b_out, sib_b_out, pull_ref = refs[7:11]
    x_ref, reg_ref, xb_ref, data_ref, sums_ref, w_ref, bias_ref, fac_ref, flg_ref, sems = refs[11:-2]
    sums = [sums_ref.at[m] for m in range(slabs - 1)] + [last_ref]
    pull_scratch = refs[-2:]
    core = place_ref[0] % 2
    rank, cols = basis_out.shape
    starts = [pl.multiple_of((place_ref[0] ^ m) * cols, cols) for m in range(slabs)]
    mine = pl.ds(pl.multiple_of(core * (fac_hbm.shape[1] // 2), series), series)
    pairs = [(x_hbm, x_ref)] + list(zip(sums_hbm, sums))
    pairs += [(reg_hbm, reg_ref), (w_hbm, w_ref), (bias_hbm, bias_ref)]
    late = [
        (fac_hbm.at[:, mine], fac_ref),
        (own_flg_hbm.at[:, mine], flg_ref.at[0]),
        (sib_flg_hbm.at[:, mine], flg_ref.at[1]),
    ]
    loads = [
        pltpu.make_async_copy(source, target, sems.at[i])
        for i, (source, target) in enumerate(pairs + late)
    ]
    for load in loads:
        load.start()
    tiles = pull_tiles(series, True)
    copies = pull_copies(core, own_hbm, sib_hbm, pull_scratch, 0, tiles)
    for load in loads[: len(pairs)]:
        load.wait()

    def step():
        xb_ref[...] = x_ref[...].astype(BF16)
        for m in range(slabs):
            for b in range(0, cols // BLK, 2):
                high, mid, low = split3(sums[m][:, cols + b * rank : cols + (b + 2) * rank])
                at = pl.multiple_of(starts[m] + b * BLK, 2 * BLK)
                xb = xb_ref[:, pl.ds(at, 2 * BLK)]
                zero = jnp.zeros((rank, BLK), BF16)
                right = jnp.concatenate(
                    [
                        jnp.concatenate([xb[:, :BLK], zero], axis=1),
                        jnp.concatenate([zero, xb[:, BLK:]], axis=1),
                    ],
                    axis=0,
                )
                got = jnp.dot(
                    jnp.concatenate([high, mid, low], axis=0), right, preferred_element_type=F32
                )
                got = got[:rank] + (got[rank : 2 * rank] + got[2 * rank :])
                data_ref[:, pl.ds(at, 2 * BLK)] = got - sums[m][:, b * BLK : (b + 2) * BLK]
        grad = data_ref[...] * data_scale + reg_ref[...]
        square = jnp.sum(grad * grad)
        x_ref[...] -= grad * (0.1 * lax.rsqrt(jnp.full((1, 1), square) / entries + 1e-06))

    def body(i, carry):
        reg_ref[...] = reg_gradient(x_ref[...], dil_ref, w_ref, bias_ref)
        step()
        return carry

    step()
    lax.fori_loop(1, ITERS, body, 0)
    basis_out[...] = x_ref[:, pl.ds(starts[0], cols)]
    own_b = x_ref[:, pl.ds(starts[0], cols)].astype(BF16)
    sib_b = x_ref[:, pl.ds(starts[1], cols)].astype(BF16)
    own_b_out[...] = own_b
    sib_b_out[...] = sib_b
    for load in loads[len(pairs) :]:
        load.wait()
    pull_chunk(
        0, tiles, copies, pull_scratch, fac_ref, flg_ref.at[0], flg_ref.at[1], own_b, sib_b,
        pull_ref,
    )


def basis_steps(
    dilations, place, weights, bias, start, sums, observed, sibling, fac_t, flags, data_scale,
    series
):
    slabs = len(sums)
    rank, total = start[0].shape
    cols = total // slabs
    smem = pl.BlockSpec(memory_space=pltpu.SMEM)
    vmem = pl.BlockSpec(memory_space=pltpu.VMEM)
    operands = [weights, bias, *sums[:-1], *start, observed, sibling, fac_t, *flags]
    kernel = functools.partial(
        steps_kernel, slabs=slabs, data_scale=data_scale, entries=float(rank * total),
        series=series,
    )
    return pl.pallas_call(
        kernel,
        in_specs=[smem, smem, vmem] + [pl.BlockSpec(memory_space=pltpu.HBM)] * len(operands),
        out_specs=[vmem] * 4,
        out_shape=[
            jax.ShapeDtypeStruct((rank, cols), F32),
            jax.ShapeDtypeStruct((rank, cols), BF16),
            jax.ShapeDtypeStruct((rank, cols), BF16),
            jax.ShapeDtypeStruct((rank, series), F32),
        ],
        scratch_shapes=[
            pltpu.VMEM((rank, total), F32),
            pltpu.VMEM((rank, total), F32),
            pltpu.VMEM((rank, total), BF16),
            pltpu.VMEM((rank, total), F32),
            pltpu.VMEM((slabs - 1, *sums[0].shape), F32),
            pltpu.VMEM(weights.shape, F32),
            pltpu.VMEM(bias.shape, F32),
            pltpu.VMEM((rank, series), BF16),
            pltpu.VMEM((2, flags[0].shape[0], series), jnp.int32),
            pltpu.SemaphoreType.DMA((slabs + 7,)),
        ]
        + pull_scratch_shapes(cols, series, pull_tiles(series, True)),
        compiler_params=pltpu.CompilerParams(vmem_limit_bytes=32 << 20),
        cost_estimate=kernel_cost(8e-6),
        name="basis_steps",
    )(
        dilations, place, pltpu.with_memory_space_constraint(sums[-1], pltpu.VMEM),
        *[in_hbm(x) for x in operands],
    )


def pull_rows(obs, fac, flg, basis):
    pred = tn_dot(fac, basis)
    resid = (pred - obs.astype(F32)).astype(BF16)
    total = None
    for b in range(flg.shape[0]):
        block = slice(b * BLK, (b + 1) * BLK)
        term = nt_dot(basis[:, block], resid[:, block]) * flg[b : b + 1, :].astype(F32)
        total = term if total is None else total + term
    return total


def pull_tiles(series, ready):
    first = series if ready or series <= PULL_ROWS else PULL_ROWS
    tiles, at = [(0, first)], first
    while at < series:
        tiles.append((at, min(3 * PULL_ROWS, series - at)))
        at += tiles[-1][1]
    return tiles


def pull_scratch_shapes(cols, series, tiles):
    return [
        pltpu.VMEM((2, series, cols), BF16),
        pltpu.SemaphoreType.DMA((len(tiles), 2)),
    ]


def pull_copies(core, own_hbm, sib_hbm, scratch, first, tiles):
    obs_ref, sems = scratch
    base = core * (own_hbm.shape[0] // 2) + first
    copies = []
    for i, (at, rows) in enumerate(tiles):
        here = pl.ds(at, rows)
        own = pl.ds(pl.multiple_of(base + at, PULL_ROWS), rows)
        copies.append(
            [
                pltpu.make_async_copy(own_hbm.at[own], obs_ref.at[0, here], sems.at[i, 0]),
                pltpu.make_async_copy(
                    sib_hbm.at[here], obs_ref.at[1, here], sems.at[i, 1]
                ),
            ]
        )
        for copy in copies[i]:
            copy.start()
    return copies


def pull_chunk(
    base, tiles, copies, scratch, fac_ref, own_flg_ref, sib_flg_ref, own_basis, sib_basis, out_ref
):
    obs_ref = scratch[0]
    for (first, height), pair in zip(tiles, copies):
        pair[0].wait()
        pair[1].wait()
        for at in range(first, first + height, 2 * PULL_ROWS):
            rows = min(2 * PULL_ROWS, first + height - at)
            here = pl.ds(at, rows)
            own = pl.ds(pl.multiple_of(base + at, PULL_ROWS), rows)
            fac = fac_ref[:, own]
            out_ref[:, here] = pull_rows(
                obs_ref[0, here, :], fac, own_flg_ref[:, own], own_basis
            ) + pull_rows(obs_ref[1, here, :], fac, sib_flg_ref[:, own], sib_basis)


def pull_kernel(
    core_ref, own_hbm, sib_hbm, fac_ref, own_flg_ref, sib_flg_ref, own_basis_ref, sib_basis_ref,
    out_ref, *scratch, first, tiles
):
    copies = pull_copies(core_ref[0], own_hbm, sib_hbm, scratch, first, tiles)
    pull_chunk(
        core_ref[0] * (fac_ref.shape[1] // 2) + first, tiles, copies, scratch, fac_ref, own_flg_ref,
        sib_flg_ref, own_basis_ref[...], sib_basis_ref[...], out_ref,
    )


def factor_pull(core, observed, sibling, fac_t, flags, basis_b, first, series):
    vmem = pl.BlockSpec(memory_space=pltpu.VMEM)
    hbm = pl.BlockSpec(memory_space=pltpu.HBM)
    tiles = pull_tiles(series, False)
    return pl.pallas_call(
        functools.partial(pull_kernel, first=first, tiles=tiles),
        in_specs=[pl.BlockSpec(memory_space=pltpu.SMEM), hbm, hbm] + [vmem] * 5,
        out_specs=vmem,
        out_shape=jax.ShapeDtypeStruct((fac_t.shape[0], series), F32),
        scratch_shapes=pull_scratch_shapes(observed.shape[1], series, tiles),
        compiler_params=pltpu.CompilerParams(vmem_limit_bytes=24 << 20),
        cost_estimate=kernel_cost(2e-6 * series / 1024),
        name="factor_pull",
    )(core, in_hbm(observed), in_hbm(sibling), fac_t, *flags, *basis_b)


def put_kernel(core_ref, *refs, places):
    pieces, (out, sems) = refs[: 2 * len(places)], refs[-2:]
    half = out.shape[1] // 2
    copies = []
    for i, ref in enumerate(pieces):
        side = core_ref[0] if i % 2 == 0 else 1 - core_ref[0]
        at = pl.multiple_of(side * half + places[i // 2], LANES)
        copies.append(
            pltpu.make_async_copy(ref, out.at[:, pl.ds(at, ref.shape[1])], sems.at[i])
        )
        copies[-1].start()
    for copy in copies:
        copy.wait()


def put(core, pieces, places, out, shape):
    old = [] if out is None else [in_hbm(out)]
    return pl.pallas_call(
        functools.partial(put_kernel, places=places),
        in_specs=[pl.BlockSpec(memory_space=pltpu.SMEM)]
        + [pl.BlockSpec(memory_space=pltpu.VMEM)] * len(pieces)
        + [pl.BlockSpec(memory_space=pltpu.HBM)] * len(old),
        out_specs=pl.BlockSpec(memory_space=pltpu.HBM),
        out_shape=pltpu.HBM(shape, BF16),
        scratch_shapes=[pltpu.SemaphoreType.DMA((len(pieces),))],
        input_output_aliases={1 + len(pieces): 0} if old else {},
        compiler_params=pltpu.CompilerParams(vmem_limit_bytes=4 << 20),
        cost_estimate=kernel_cost(1e-6),
        name="put",
    )(core, *pieces, *old)


def swap(x, axis, bit):
    count = lax.axis_size(axis)
    return lax.ppermute(x, axis, [(i, i ^ bit) for i in range(count)])


def sum_over(x, axis, beside):
    count = lax.axis_size(axis)
    if count & (count - 1):
        return lax.psum(x, axis)
    bit = 1
    while bit < count:
        other = swap(x, axis, bit)
        if beside:
            done = beside.pop(0)(x)
            x = after(x + other, *done)
        else:
            x = x + other
        bit *= 2
    return x


def after(x, *others):
    return lax.optimization_barrier((x, *others))[0]


def shards(observed, flags, factors, basis, tcn_weights, tcn_bias, dilations):
    series, cols = observed.shape
    half = series // 2
    time_count = lax.axis_size("tm")
    place = lax.axis_index("tm")
    core = (place % 2).astype(jnp.int32).reshape(1)
    fac_t, flg_t = factors.T, flags.T
    data_scale = 1.0 / math.sqrt(series * lax.axis_size("series"))
    coef = 0.1 / math.sqrt(cols * time_count)

    place = place.astype(jnp.int32).reshape(1)
    unit = half // sum(CHUNKS)

    slabs, parts, siblings = {0: basis}, [], []

    def beside_1(now):
        parts.append(other_part(after(core, now), observed, 0, CHUNKS[0] * unit))
        return parts[:]

    def beside_2(now):
        siblings.append(swap(after(parts[0], now), "tm", 1))
        slabs[2] = swap(after(basis, now), "tm", 2)
        parts.append(
            other_part(after(core, now), observed, CHUNKS[0] * unit, CHUNKS[1] * unit)
        )
        return [slabs[2], parts[1]]

    def beside_3(now):
        siblings.append(swap(after(parts[1], now), "tm", 1))
        slabs[1] = swap(after(basis, now), "tm", 1)
        slabs[3] = swap(after(slabs[2], now), "tm", 1)
        slabs["flags"] = swap(after(flg_t, now), "tm", 1)
        return [slabs[1], slabs[3]]

    beside = [beside_1, beside_2, beside_3]
    sums = sum_over(gram(observed, fac_t, flg_t, 1024), "series", beside)
    for work in beside:
        work(sums)
    flags = (flg_t, slabs["flags"])
    start = network_start(
        dilations, after(place, sums), tcn_weights, tcn_bias, [slabs[m] for m in range(time_count)]
    )
    far = after(swap(sums, "tm", 2), start[1])
    sums = [sums, swap(sums, "tm", 1), far, swap(far, "tm", 1)]
    new_basis, own_b, sib_b, pull = basis_steps(
        dilations, place, tcn_weights, tcn_bias, start, sums,
        observed, siblings[0], fac_t, flags, data_scale, CHUNKS[0] * unit,
    )
    sent, arrived, pieces, firsts = [], [], [], []
    first = 0
    for c, chunk in enumerate(CHUNKS):
        width = chunk * unit
        if c > 0:
            own_b = after(own_b, *sent)
            pull = factor_pull(
                core, observed, siblings[1], fac_t, flags, (own_b, sib_b), first, width
            )
        own = (pull * coef).astype(jnp.float16)
        at = 0
        for cut in CUTS[c]:
            piece = own[:, at * unit : (at + cut) * unit]
            if c > 0:
                piece = after(piece, arrived[0])
            sent.append(piece)
            arrived.append(swap(piece, "tm", 2))
            firsts.append(first + at * unit)
            at += cut
        first += width
    early = len(CUTS[0])
    for c, (own, got) in enumerate(zip(sent, arrived)):
        if c < early:
            got = after(got, *sent[early:])
        if c == early:
            new_factors = put(core, pieces, firsts[:early], None, fac_t.shape)
            pieces = []
        if c >= early:
            got = after(got, new_factors)
        both = own.astype(F32) + got.astype(F32)
        mine = lax.dynamic_slice_in_dim(fac_t, core[0] * half + firsts[c], own.shape[1], 1)
        new = (mine.astype(F32) - both).astype(BF16)
        pieces += [new, swap(new, "tm", 1)]
    new_factors = put(core, pieces, firsts[early:], new_factors, fac_t.shape)
    return new_basis, new_factors.T


def solution(mesh):
    return jax.shard_map(
        shards,
        mesh=mesh,
        in_specs=(
            P("series", "tm"),
            P("series", "tm"),
            P("series", None),
            P(None, "tm"),
            P(),
            P(),
            P(),
        ),
        out_specs=(P(None, "tm"), P("series", None)),
        check_vma=False,
    )
```

```python
import functools
import math

import jax
import jax.numpy as jnp
from jax import lax
from jax.experimental import pallas as pl
from jax.experimental.pallas import tpu as pltpu
from jax.sharding import PartitionSpec as P

BLK = 128
LANES = 128
ITERS = 3
VMEM_BYTES = 40 << 20
SMALL_BYTES = 24 << 20
PULL_ROWS = 1024
SCALE = 4.0
CHUNKS = (4, 4)
CUTS = ((2, 2), (3, 1))
F32 = jnp.float32
BF16 = jnp.bfloat16


def nt_dot(a, b):
    return lax.dot_general(a, b, (((1,), (1,)), ((), ())), preferred_element_type=F32)


def tn_dot(a, b):
    return lax.dot_general(a, b, (((0,), (0,)), ((), ())), preferred_element_type=F32)


def kernel_cost(seconds):
    return pl.CostEstimate(flops=0, bytes_accessed=int(seconds * 3.69e12), transcendentals=0)


def gram_kernel(
    obs_hbm, fac_hbm, flg_hbm, out_ref, obs_ref, fac_ref, flg_ref, sems, *, rows
):
    series = obs_ref.shape[0]
    rank, blocks = fac_ref.shape[0], flg_ref.shape[0]
    flg_copy = pltpu.make_async_copy(flg_hbm, flg_ref, sems.at[0])
    flg_copy.start()
    steps = series // rows
    fac_copies, copies = [], []
    for i in range(steps):
        if i % (steps // 2) == 0:
            cut = pl.ds(i * rows, series // 2)
            fac_copies.append(
                pltpu.make_async_copy(
                    fac_hbm.at[:, cut], fac_ref.at[:, cut], sems.at[1 + len(fac_copies)]
                )
            )
            fac_copies[-1].start()
        cut = pl.ds(i * rows, rows)
        copies.append(pltpu.make_async_copy(obs_hbm.at[cut], obs_ref.at[cut], sems.at[3 + i]))
        copies[i].start()
    flg_copy.wait()
    for i, copy in enumerate(copies):
        if i % (steps // 2) == 0:
            fac_copies[i // (steps // 2)].wait()
        cut = pl.ds(i * rows, rows)
        fac = fac_ref[:, cut]
        flg = flg_ref[:, cut].astype(F32).astype(BF16)
        masked = jnp.concatenate([fac * flg[b : b + 1, :] for b in range(blocks)], axis=0)
        gram_part = nt_dot(fac, masked)
        copy.wait()
        parts = []
        for b in range(0, blocks, 2):
            both = jnp.dot(
                masked[b * rank : (b + 2) * rank],
                obs_ref[cut, b * BLK : (b + 2) * BLK],
                preferred_element_type=F32,
            )
            parts += [both[:rank, :BLK], both[rank:, BLK:]]
        new = jnp.concatenate(parts + [gram_part], axis=1)
        if i == 0:
            out_ref[...] = new
        else:
            out_ref[...] += new


def part_kernel(core_ref, obs_hbm, out_hbm, part_ref, sems, *, first, pieces):
    rows = out_hbm.shape[0] // pieces
    base = (1 - core_ref[0]) * (obs_hbm.shape[0] // 2) + first
    loads, stores = [], []
    for i in range(pieces):
        here = pl.ds(i * rows, rows)
        there = pl.ds(pl.multiple_of(base + i * rows, rows), rows)
        loads.append(pltpu.make_async_copy(obs_hbm.at[there], part_ref.at[here], sems.at[i, 0]))
        stores.append(pltpu.make_async_copy(part_ref.at[here], out_hbm.at[here], sems.at[i, 1]))
    for load in loads:
        load.start()
    for load, store in zip(loads, stores):
        load.wait()
        store.start()
    for store in stores:
        store.wait()


def other_part(core, observed, first, rows):
    hbm = pl.BlockSpec(memory_space=pltpu.HBM)
    pieces = 8
    return pl.pallas_call(
        functools.partial(part_kernel, first=first, pieces=pieces),
        in_specs=[pl.BlockSpec(memory_space=pltpu.SMEM), hbm],
        out_specs=hbm,
        out_shape=pltpu.HBM((rows, observed.shape[1]), observed.dtype),
        scratch_shapes=[
            pltpu.VMEM((rows, observed.shape[1]), observed.dtype),
            pltpu.SemaphoreType.DMA((pieces, 2)),
        ],
        compiler_params=pltpu.CompilerParams(vmem_limit_bytes=16 << 20),
        cost_estimate=kernel_cost(3e-6),
        name="other_part",
    )(core, in_hbm(observed))


def in_hbm(x):
    return pltpu.with_memory_space_constraint(x, pltpu.HBM)


def gram(observed, fac_t, flg_t, rows):
    series, cols = observed.shape
    rank, blocks = fac_t.shape[0], flg_t.shape[0]
    width = cols + blocks * rank
    hbm = pl.BlockSpec(memory_space=pltpu.HBM)
    return pl.pallas_call(
        functools.partial(gram_kernel, rows=rows),
        in_specs=[hbm, hbm, hbm],
        out_specs=pl.BlockSpec(memory_space=pltpu.VMEM),
        out_shape=jax.ShapeDtypeStruct((rank, width), F32),
        scratch_shapes=[
            pltpu.VMEM((series, cols), BF16),
            pltpu.VMEM(fac_t.shape, BF16),
            pltpu.VMEM(flg_t.shape, jnp.int32),
            pltpu.SemaphoreType.DMA((3 + series // rows,)),
        ],
        compiler_params=pltpu.CompilerParams(vmem_limit_bytes=32 << 20),
        cost_estimate=kernel_cost(8e-6),
        name="gram",
    )(in_hbm(observed), in_hbm(fac_t), in_hbm(flg_t))


def split(x):
    high = x.astype(BF16)
    return high, (x - high.astype(F32)).astype(BF16)


def split3(x):
    high, mid = split(x)
    return high, mid, (x - high.astype(F32) - mid.astype(F32)).astype(BF16)


def later(x, steps, fill):
    lane = lax.broadcasted_iota(jnp.int32, (x.shape[0], LANES), 1)
    before = jnp.broadcast_to(fill, (x.shape[0], LANES))
    out = []
    for j in range(0, x.shape[1], LANES):
        rolled = pltpu.roll(x[:, j : j + LANES], steps, 1)
        out.append(jnp.where(lane < steps, before, rolled))
        before = rolled
    return jnp.concatenate(out, axis=1)


def earlier(x, steps):
    lane = lax.broadcasted_iota(jnp.int32, (x.shape[0], LANES), 1)
    rolled = [
        pltpu.roll(x[:, j : j + LANES], LANES - steps, 1) for j in range(0, x.shape[1], LANES)
    ]
    rolled.append(jnp.zeros((x.shape[0], LANES), F32))
    out = [jnp.where(lane < LANES - steps, a, b) for a, b in zip(rolled[:-1], rolled[1:])]
    return jnp.concatenate(out, axis=1)


def taps(first, second):
    fh, fl = split(first)
    sh, sl = split(second)
    zero = jnp.zeros_like(fh)
    top = jnp.concatenate([fh, sh, fh, sh], axis=1)
    bottom = jnp.concatenate([fl, sl, zero, zero], axis=1)
    return jnp.concatenate([top, bottom], axis=0)


def pair_dot(weights, a, b):
    ah, al = split(a)
    bh, bl = split(b)
    both = jnp.dot(
        weights, jnp.concatenate([ah, bh, al, bl], axis=0), preferred_element_type=F32
    )
    rank = a.shape[0]
    return both[:rank] + both[rank:]


def column(row):
    shape = (row.shape[1], row.shape[1])
    same = lax.broadcasted_iota(jnp.int32, shape, 0) == lax.broadcasted_iota(jnp.int32, shape, 1)
    return jnp.sum(jnp.where(same, jnp.broadcast_to(row, shape), 0.0), axis=1, keepdims=True)


def reg_gradient(x, dil_ref, w_ref, bias_ref):
    d0, d1 = dil_ref[0], dil_ref[1]
    b0, b1 = column(bias_ref[0:1, :]), column(bias_ref[1:2, :])
    w = [w_ref[i] for i in range(4)]
    z = later(x, 1, 0.0)
    pre = pair_dot(taps(w[0], w[1]), later(z, d0, 0.0), z) + b0
    hidden = jnp.maximum(pre, 0.0)
    shown = later(hidden, d1, jnp.maximum(b0, 0.0))
    error = 0.1 * (x - z - pair_dot(taps(w[2], w[3]), shown, hidden) - b1)
    pull = -pair_dot(taps(w[2].T, w[3].T), earlier(error, d1), error)
    pull = jnp.where(pre > 0.0, pull, 0.0)
    back = pair_dot(taps(w[0].T, w[1].T), earlier(pull, d0), pull)
    return error + earlier(back - error, 1)


def network_kernel(dil_ref, place_ref, w_hbm, bias_hbm, *refs, slabs):
    basis_hbm, (x_hbm, reg_hbm, x_ref, reg_ref, w_ref, bias_ref, sems) = refs[:slabs], refs[slabs:]
    cols = basis_hbm[0].shape[1]
    pairs = [(w_hbm, w_ref), (bias_hbm, bias_ref)]
    for m in range(slabs):
        start = pl.multiple_of((place_ref[0] ^ m) * cols, cols)
        pairs.append((basis_hbm[m], x_ref.at[:, pl.ds(start, cols)]))
    loads = [
        pltpu.make_async_copy(source, target, sems.at[i])
        for i, (source, target) in enumerate(pairs)
    ]
    for load in loads:
        load.start()
    for load in loads:
        load.wait()
    x_store = pltpu.make_async_copy(x_ref, x_hbm, sems.at[slabs + 2])
    reg_store = pltpu.make_async_copy(reg_ref, reg_hbm, sems.at[slabs + 3])
    x_store.start()
    reg_ref[...] = reg_gradient(x_ref[...], dil_ref, w_ref, bias_ref)
    reg_store.start()
    x_store.wait()
    reg_store.wait()


def network_start(dilations, place, weights, bias, basis):
    slabs = len(basis)
    rank, cols = basis[0].shape
    smem = pl.BlockSpec(memory_space=pltpu.SMEM)
    hbm = pl.BlockSpec(memory_space=pltpu.HBM)
    whole = (rank, slabs * cols)
    return pl.pallas_call(
        functools.partial(network_kernel, slabs=slabs),
        in_specs=[smem, smem] + [hbm] * (2 + slabs),
        out_specs=[hbm, hbm],
        out_shape=[pltpu.HBM(whole, F32), pltpu.HBM(whole, F32)],
        scratch_shapes=[
            pltpu.VMEM(whole, F32),
            pltpu.VMEM(whole, F32),
            pltpu.VMEM(weights.shape, F32),
            pltpu.VMEM(bias.shape, F32),
            pltpu.SemaphoreType.DMA((slabs + 4,)),
        ],
        compiler_params=pltpu.CompilerParams(vmem_limit_bytes=16 << 20),
        cost_estimate=kernel_cost(3e-6),
        name="network_start",
    )(dilations, place, *[in_hbm(x) for x in (weights, bias, *basis)])


def steps_kernel(
    dil_ref, place_ref, last_ref, w_hbm, bias_hbm, *refs, slabs, data_scale, entries, series
):
    sums_hbm, refs = refs[: slabs - 1], refs[slabs - 1 :]
    x_hbm, reg_hbm, own_hbm, sib_hbm, fac_hbm, own_flg_hbm, sib_flg_hbm = refs[:7]
    basis_out, own_b_out, sib_b_out, pull_ref = refs[7:11]
    x_ref, reg_ref, xb_ref, data_ref, sums_ref, w_ref, bias_ref, fac_ref, flg_ref, sems = refs[11:-2]
    sums = [sums_ref.at[m] for m in range(slabs - 1)] + [last_ref]
    pull_scratch = refs[-2:]
    core = place_ref[0] % 2
    rank, cols = basis_out.shape
    starts = [pl.multiple_of((place_ref[0] ^ m) * cols, cols) for m in range(slabs)]
    mine = pl.ds(pl.multiple_of(core * (fac_hbm.shape[1] // 2), series), series)
    pairs = [(x_hbm, x_ref)] + list(zip(sums_hbm, sums))
    pairs += [(reg_hbm, reg_ref), (w_hbm, w_ref), (bias_hbm, bias_ref)]
    late = [
        (fac_hbm.at[:, mine], fac_ref),
        (own_flg_hbm.at[:, mine], flg_ref.at[0]),
        (sib_flg_hbm.at[:, mine], flg_ref.at[1]),
    ]
    loads = [
        pltpu.make_async_copy(source, target, sems.at[i])
        for i, (source, target) in enumerate(pairs + late)
    ]
    for load in loads:
        load.start()
    tiles = pull_tiles(series, True)
    copies = pull_copies(core, own_hbm, sib_hbm, pull_scratch, 0, tiles)
    for load in loads[: len(pairs)]:
        load.wait()

    def step():
        xb_ref[...] = x_ref[...].astype(BF16)
        for m in range(slabs):
            for b in range(0, cols // BLK, 2):
                high, mid, low = split3(sums[m][:, cols + b * rank : cols + (b + 2) * rank])
                at = pl.multiple_of(starts[m] + b * BLK, 2 * BLK)
                xb = xb_ref[:, pl.ds(at, 2 * BLK)]
                zero = jnp.zeros((rank, BLK), BF16)
                right = jnp.concatenate(
                    [
                        jnp.concatenate([xb[:, :BLK], zero], axis=1),
                        jnp.concatenate([zero, xb[:, BLK:]], axis=1),
                    ],
                    axis=0,
                )
                got = jnp.dot(
                    jnp.concatenate([high, mid, low], axis=0), right, preferred_element_type=F32
                )
                got = got[:rank] + (got[rank : 2 * rank] + got[2 * rank :])
                data_ref[:, pl.ds(at, 2 * BLK)] = got - sums[m][:, b * BLK : (b + 2) * BLK]
        grad = data_ref[...] * data_scale + reg_ref[...]
        square = jnp.sum(grad * grad)
        x_ref[...] -= grad * (0.1 * lax.rsqrt(jnp.full((1, 1), square) / entries + 1e-06))

    def body(i, carry):
        reg_ref[...] = reg_gradient(x_ref[...], dil_ref, w_ref, bias_ref)
        step()
        return carry

    step()
    lax.fori_loop(1, ITERS, body, 0)
    basis_out[...] = x_ref[:, pl.ds(starts[0], cols)]
    own_b = x_ref[:, pl.ds(starts[0], cols)].astype(BF16)
    sib_b = x_ref[:, pl.ds(starts[1], cols)].astype(BF16)
    own_b_out[...] = own_b
    sib_b_out[...] = sib_b
    for load in loads[len(pairs) :]:
        load.wait()
    pull_chunk(
        0, tiles, copies, pull_scratch, fac_ref, flg_ref.at[0], flg_ref.at[1], own_b, sib_b,
        pull_ref,
    )


def basis_steps(
    dilations, place, weights, bias, start, sums, observed, sibling, fac_t, flags, data_scale,
    series
):
    slabs = len(sums)
    rank, total = start[0].shape
    cols = total // slabs
    smem = pl.BlockSpec(memory_space=pltpu.SMEM)
    vmem = pl.BlockSpec(memory_space=pltpu.VMEM)
    operands = [weights, bias, *sums[:-1], *start, observed, sibling, fac_t, *flags]
    kernel = functools.partial(
        steps_kernel, slabs=slabs, data_scale=data_scale, entries=float(rank * total),
        series=series,
    )
    return pl.pallas_call(
        kernel,
        in_specs=[smem, smem, vmem] + [pl.BlockSpec(memory_space=pltpu.HBM)] * len(operands),
        out_specs=[vmem] * 4,
        out_shape=[
            jax.ShapeDtypeStruct((rank, cols), F32),
            jax.ShapeDtypeStruct((rank, cols), BF16),
            jax.ShapeDtypeStruct((rank, cols), BF16),
            jax.ShapeDtypeStruct((rank, series), F32),
        ],
        scratch_shapes=[
            pltpu.VMEM((rank, total), F32),
            pltpu.VMEM((rank, total), F32),
            pltpu.VMEM((rank, total), BF16),
            pltpu.VMEM((rank, total), F32),
            pltpu.VMEM((slabs - 1, *sums[0].shape), F32),
            pltpu.VMEM(weights.shape, F32),
            pltpu.VMEM(bias.shape, F32),
            pltpu.VMEM((rank, series), BF16),
            pltpu.VMEM((2, flags[0].shape[0], series), jnp.int32),
            pltpu.SemaphoreType.DMA((slabs + 7,)),
        ]
        + pull_scratch_shapes(cols, series, pull_tiles(series, True)),
        compiler_params=pltpu.CompilerParams(vmem_limit_bytes=32 << 20),
        cost_estimate=kernel_cost(8e-6),
        name="basis_steps",
    )(
        dilations, place, pltpu.with_memory_space_constraint(sums[-1], pltpu.VMEM),
        *[in_hbm(x) for x in operands],
    )


def pull_rows(obs, fac, flg, basis):
    pred = tn_dot(fac, basis)
    resid = (pred - obs.astype(F32)).astype(BF16)
    total = None
    for b in range(flg.shape[0]):
        block = slice(b * BLK, (b + 1) * BLK)
        term = nt_dot(basis[:, block], resid[:, block]) * flg[b : b + 1, :].astype(F32)
        total = term if total is None else total + term
    return total


def pull_tiles(series, ready):
    first = series if ready or series <= PULL_ROWS else PULL_ROWS
    tiles, at = [(0, first)], first
    while at < series:
        tiles.append((at, min(3 * PULL_ROWS, series - at)))
        at += tiles[-1][1]
    return tiles


def pull_scratch_shapes(cols, series, tiles):
    return [
        pltpu.VMEM((2, series, cols), BF16),
        pltpu.SemaphoreType.DMA((len(tiles), 2)),
    ]


def pull_copies(core, own_hbm, sib_hbm, scratch, first, tiles):
    obs_ref, sems = scratch
    base = core * (own_hbm.shape[0] // 2) + first
    copies = []
    for i, (at, rows) in enumerate(tiles):
        here = pl.ds(at, rows)
        own = pl.ds(pl.multiple_of(base + at, PULL_ROWS), rows)
        copies.append(
            [
                pltpu.make_async_copy(own_hbm.at[own], obs_ref.at[0, here], sems.at[i, 0]),
                pltpu.make_async_copy(
                    sib_hbm.at[here], obs_ref.at[1, here], sems.at[i, 1]
                ),
            ]
        )
        for copy in copies[i]:
            copy.start()
    return copies


def pull_chunk(
    base, tiles, copies, scratch, fac_ref, own_flg_ref, sib_flg_ref, own_basis, sib_basis, out_ref
):
    obs_ref = scratch[0]
    for (first, height), pair in zip(tiles, copies):
        pair[0].wait()
        pair[1].wait()
        for at in range(first, first + height, 2 * PULL_ROWS):
            rows = min(2 * PULL_ROWS, first + height - at)
            here = pl.ds(at, rows)
            own = pl.ds(pl.multiple_of(base + at, PULL_ROWS), rows)
            fac = fac_ref[:, own]
            out_ref[:, here] = pull_rows(
                obs_ref[0, here, :], fac, own_flg_ref[:, own], own_basis
            ) + pull_rows(obs_ref[1, here, :], fac, sib_flg_ref[:, own], sib_basis)


def pull_kernel(
    core_ref, own_hbm, sib_hbm, fac_hbm, own_flg_hbm, sib_flg_hbm, own_basis_ref, sib_basis_ref,
    out_ref, fac_ref, flg_ref, sems, *scratch, first, tiles
):
    series = out_ref.shape[1]
    base = pl.multiple_of(core_ref[0] * (fac_hbm.shape[1] // 2) + first, PULL_ROWS)
    mine = pl.ds(base, series)
    loads = [
        pltpu.make_async_copy(own_flg_hbm.at[:, mine], flg_ref.at[0], sems.at[0]),
        pltpu.make_async_copy(sib_flg_hbm.at[:, mine], flg_ref.at[1], sems.at[1]),
        pltpu.make_async_copy(fac_hbm.at[:, mine], fac_ref, sems.at[2]),
    ]
    for load in loads:
        load.start()
    copies = pull_copies(core_ref[0], own_hbm, sib_hbm, scratch, first, tiles)
    for load in loads:
        load.wait()
    pull_chunk(
        0, tiles, copies, scratch, fac_ref, flg_ref.at[0], flg_ref.at[1], own_basis_ref[...],
        sib_basis_ref[...], out_ref,
    )


def factor_pull(core, observed, sibling, fac_t, flags, basis_b, first, series):
    rank, blocks = fac_t.shape[0], flags[0].shape[0]
    vmem = pl.BlockSpec(memory_space=pltpu.VMEM)
    hbm = pl.BlockSpec(memory_space=pltpu.HBM)
    tiles = pull_tiles(series, False)
    return pl.pallas_call(
        functools.partial(pull_kernel, first=first, tiles=tiles),
        in_specs=[pl.BlockSpec(memory_space=pltpu.SMEM)] + [hbm] * 5 + [vmem] * 2,
        out_specs=vmem,
        out_shape=jax.ShapeDtypeStruct((rank, series), F32),
        scratch_shapes=[
            pltpu.VMEM((rank, series), BF16),
            pltpu.VMEM((2, blocks, series), jnp.int32),
            pltpu.SemaphoreType.DMA((3,)),
        ]
        + pull_scratch_shapes(observed.shape[1], series, tiles),
        compiler_params=pltpu.CompilerParams(vmem_limit_bytes=24 << 20),
        cost_estimate=kernel_cost(2e-6 * series / 1024),
        name="factor_pull",
    )(core, *[in_hbm(x) for x in (observed, sibling, fac_t, *flags)], *basis_b)


def put_kernel(core_ref, *refs, places):
    pieces, (out, sems) = refs[: 2 * len(places)], refs[-2:]
    half = out.shape[1] // 2
    copies = []
    for i, ref in enumerate(pieces):
        side = core_ref[0] if i % 2 == 0 else 1 - core_ref[0]
        at = pl.multiple_of(side * half + places[i // 2], LANES)
        copies.append(
            pltpu.make_async_copy(ref, out.at[:, pl.ds(at, ref.shape[1])], sems.at[i])
        )
        copies[-1].start()
    for copy in copies:
        copy.wait()


def put(core, pieces, places, out, shape):
    old = [] if out is None else [in_hbm(out)]
    return pl.pallas_call(
        functools.partial(put_kernel, places=places),
        in_specs=[pl.BlockSpec(memory_space=pltpu.SMEM)]
        + [pl.BlockSpec(memory_space=pltpu.VMEM)] * len(pieces)
        + [pl.BlockSpec(memory_space=pltpu.HBM)] * len(old),
        out_specs=pl.BlockSpec(memory_space=pltpu.HBM),
        out_shape=pltpu.HBM(shape, BF16),
        scratch_shapes=[pltpu.SemaphoreType.DMA((len(pieces),))],
        input_output_aliases={1 + len(pieces): 0} if old else {},
        compiler_params=pltpu.CompilerParams(vmem_limit_bytes=4 << 20),
        cost_estimate=kernel_cost(1e-6),
        name="put",
    )(core, *pieces, *old)


def swap(x, axis, bit):
    count = lax.axis_size(axis)
    return lax.ppermute(x, axis, [(i, i ^ bit) for i in range(count)])


def sum_over(x, axis, beside):
    count = lax.axis_size(axis)
    if count & (count - 1):
        return lax.psum(x, axis)
    bit = 1
    while bit < count:
        other = swap(x, axis, bit)
        if beside:
            done = beside.pop(0)(x)
            x = after(x + other, *done)
        else:
            x = x + other
        bit *= 2
    return x


def after(x, *others):
    return lax.optimization_barrier((x, *others))[0]


def shards(observed, flags, factors, basis, tcn_weights, tcn_bias, dilations):
    series, cols = observed.shape
    half = series // 2
    time_count = lax.axis_size("tm")
    place = lax.axis_index("tm")
    core = (place % 2).astype(jnp.int32).reshape(1)
    fac_t, flg_t = factors.T, flags.T
    data_scale = 1.0 / math.sqrt(series * lax.axis_size("series"))
    coef = 0.1 / math.sqrt(cols * time_count)

    place = place.astype(jnp.int32).reshape(1)
    unit = half // sum(CHUNKS)

    slabs, parts, siblings = {0: basis}, [], []

    def beside_1(now):
        parts.append(other_part(after(core, now), observed, 0, CHUNKS[0] * unit))
        return parts[:]

    def beside_2(now):
        siblings.append(swap(after(parts[0], now), "tm", 1))
        slabs[2] = swap(after(basis, now), "tm", 2)
        parts.append(
            other_part(after(core, now), observed, CHUNKS[0] * unit, CHUNKS[1] * unit)
        )
        return [slabs[2], parts[1]]

    def beside_3(now):
        siblings.append(swap(after(parts[1], now), "tm", 1))
        slabs[1] = swap(after(basis, now), "tm", 1)
        slabs[3] = swap(after(slabs[2], now), "tm", 1)
        slabs["flags"] = swap(after(flg_t, now), "tm", 1)
        return [slabs[1], slabs[3]]

    beside = [beside_1, beside_2, beside_3]
    sums = sum_over(gram(observed, fac_t, flg_t, 1024), "series", beside)
    for work in beside:
        work(sums)
    flags = (flg_t, slabs["flags"])
    start = network_start(
        dilations, after(place, sums), tcn_weights, tcn_bias, [slabs[m] for m in range(time_count)]
    )
    far = after(swap(sums, "tm", 2), start[1])
    sums = [sums, swap(sums, "tm", 1), far, swap(far, "tm", 1)]
    new_basis, own_b, sib_b, pull = basis_steps(
        dilations, place, tcn_weights, tcn_bias, start, sums,
        observed, siblings[0], fac_t, flags, data_scale, CHUNKS[0] * unit,
    )
    sent, arrived, pieces, firsts = [], [], [], []
    first = 0
    for c, chunk in enumerate(CHUNKS):
        width = chunk * unit
        if c > 0:
            own_b = after(own_b, *sent)
            pull = factor_pull(
                core, observed, siblings[1], fac_t, flags, (own_b, sib_b), first, width
            )
        at = 0
        for cut in CUTS[c]:
            piece = (pull[:, at * unit : (at + cut) * unit] * (SCALE * coef)).astype(jnp.float16)
            if c > 0:
                piece = after(piece, arrived[0])
            sent.append(piece)
            arrived.append(swap(piece, "tm", 2))
            firsts.append(first + at * unit)
            at += cut
        first += width
    early = len(CUTS[0])
    for c, (own, got) in enumerate(zip(sent, arrived)):
        if c < early:
            got = after(got, *sent[early:])
        if c == early:
            new_factors = put(core, pieces, firsts[:early], None, fac_t.shape)
            pieces = []
        if c >= early:
            got = after(got, new_factors)
        both = own.astype(F32) + got.astype(F32)
        mine = lax.dynamic_slice_in_dim(fac_t, core[0] * half + firsts[c], own.shape[1], 1)
        new = (mine.astype(F32) - both * (1.0 / SCALE)).astype(BF16)
        pieces += [new, swap(new, "tm", 1)]
    new_factors = put(core, pieces, firsts[early:], new_factors, fac_t.shape)
    return new_basis, new_factors.T


def solution(mesh):
    return jax.shard_map(
        shards,
        mesh=mesh,
        in_specs=(
            P("series", "tm"),
            P("series", "tm"),
            P("series", None),
            P(None, "tm"),
            P(),
            P(),
            P(),
        ),
        out_specs=(P(None, "tm"), P("series", None)),
        check_vma=False,
    )
```
